32 devices in a mesh: sp: 8 (over z, x), hd: 4 (over y, core).
Axes of the slice: x: 2, y: 2, z: 4, core: 2. Of those that a mesh axis runs over, the one named last changes fastest.
Arguments:
- tokens: bfloat16 [4096, 2304], P(('sp', 'hd')), may hold values from -6 to 6
- gains: float32 [4, 2304], replicated, may hold values from -0.5 to 0.5
- w_qkv: bfloat16 [2304, 4096], P(('sp', 'hd')), may hold values from -0.1875 to 0.1875
- w_out: bfloat16 [2304, 2048], P(('sp', 'hd')), may hold values from -0.125 to 0.125
- w_in: bfloat16 [2304, 18432], P(('sp', 'hd')), may hold values from -0.125 to 0.125
- w_down: bfloat16 [2304, 9216], P(('sp', 'hd')), may hold values from -0.0625 to 0.0625
- lengths: int32 [16], replicated, may hold values from 1 to 2048, 4096 in all
- cotangent: bfloat16 [4096, 2304], P(('sp', 'hd')), may hold values from -6 to 6
Outputs:
- result: bfloat16 [4096, 2304], P(('sp', 'hd'))
- grad_tokens: float32 [4096, 2304], P(('sp', 'hd'))
- grad_qkv: float32 [2304, 4096], P(('sp', 'hd'))
- grad_out: float32 [2304, 2048], P(('sp', 'hd'))
- grad_in: float32 [2304, 18432], P(('sp', 'hd'))
- grad_down: float32 [2304, 9216], P(('sp', 'hd'))
- grad_gains: float32 [4, 2304], replicated
- column_scales: float32 [22528], replicated
- row_scales: float32 [2, 2304], P(None, ('sp', 'hd'))
The draws below stay inside these ranges and needn't reach their ends.
Inputs may be any that keep to these rules, and one draw needn't show every extreme that they name: `lengths`: they sum to 4096 and the longest is exactly 2048.
All inputs are finite; a program needn't handle non-finite values.
Results may differ from the reference program's by a relative error of at most 0.02.
Values may be sent and summed in bfloat16 or wider, within the bound.
No kernel may reach another device: no remote copies, remote signals or barrier semaphores. Data moves between devices by JAX's collectives and lax.ppermute only.
A program may use at most 640 MiB of HBM per device.

```python
import math
import jax
import jax.numpy as jnp
import numpy as np
from jax import lax

D = 2304
FF = 9216
QH = 8
KVH = 4
HD = 256
WINDOW = 4096
NDOCS = 16
TOKENS = 4096
SHARD = 512
DOC_MOST = 2048
G = 2
QD = 2048
QKVW = 4096


def levels(rng, extent, split, low, top_value):
    loudness, own = 1.0, jax.random.fold_in(rng, 6)
    for dim, blocks in split:
        heights = jnp.exp(jax.random.uniform(jax.random.fold_in(own, dim), (blocks,), jnp.float32, low / len(split), top_value / len(split)))
        loudness = loudness * jnp.repeat(heights, extent[dim] // blocks).reshape([-1 if axis == dim else 1 for axis in range(len(extent))])
    return loudness


def split_up(amount, total, reach, slope):
    loads = [(1 << 20) // math.isqrt(standing ** slope) + 1 for standing in range(2, amount + 1)]
    rest, holding = total - reach - (amount - 1), [1] * (amount - 1)
    while rest > 0:
        free = [i for i in range(amount - 1) if holding[i] < reach]
        whole, budget = sum([loads[i] for i in free]), rest
        for i in free:
            addition = min(reach - holding[i], max(1, budget * loads[i] // whole), rest)
            holding[i] = holding[i] + addition
            rest = rest - addition
    return np.array([reach] + holding)


def ragged(own_key, count, total, reach, slope):
    if count == 2:
        one = jax.random.randint(own_key, (), max(1, total - reach), min(reach, total - 1) + 1)
        return jnp.stack([one, total - one])
    sizes = jnp.asarray(split_up(count, total, reach, slope), jnp.int32)
    couples = (count - 1) // 2
    source_of, taker = sizes[1:1 + 2 * couples:2], sizes[2:2 + 2 * couples:2]
    margin = jnp.minimum(source_of - 1, reach - taker)
    passed = jax.random.randint(jax.random.fold_in(own_key, 1), (couples,), 0, 1 << 20) % (margin + 1)
    sizes = sizes.at[1:1 + 2 * couples:2].set(source_of - passed).at[2:2 + 2 * couples:2].set(taker + passed)
    return sizes[jax.random.permutation(jax.random.fold_in(own_key, 2), count)]


def gaussian(key, shape, deviation, most, cuts=(), kind=jnp.bfloat16):
    loudness = levels(key, shape, cuts, -0.22, 0.18) if cuts else 1.0
    values = jax.random.normal(key, shape, jnp.float32) * deviation * loudness
    return jnp.minimum(jnp.maximum(values, -most), most).astype(kind)


def setup_inputs(seed: int = 0) -> dict:
    key_list = jax.random.split(jax.random.key(seed), 9)
    tokens = gaussian(key_list[0], (TOKENS, D), 1.0, 6.0, ((0, 32),))
    gains = jnp.clip(jax.random.uniform(key_list[1], (4, D), jnp.float32, -0.5, 0.5), -0.5, 0.5)
    w_qkv = gaussian(key_list[2], (D, QKVW), (D // 2) ** -0.5, 0.1875, ((0, 32),))
    w_out = gaussian(key_list[3], (D, QD), QD ** -0.5, 0.125, ((0, 32),))
    w_in = gaussian(key_list[4], (D, 2 * FF), D ** -0.5, 0.125, ((0, 32),))
    w_down = gaussian(key_list[5], (D, FF), FF ** -0.5, 0.0625, ((0, 32),))
    lengths = ragged(key_list[6], NDOCS, TOKENS, DOC_MOST, 2).astype(jnp.int32)
    cotangent = gaussian(key_list[7], (TOKENS, D), 1.0, 6.0, ((0, 32),))
    return {"tokens": tokens, "gains": gains, "w_qkv": w_qkv, "w_out": w_out, "w_in": w_in, "w_down": w_down, "lengths": lengths, "cotangent": cotangent}


@jax.custom_vjp
def low(v):
    return lax.optimization_barrier(v.astype(jnp.bfloat16)).astype(jnp.float32)

@jax.custom_vjp
def low_back(v):
    return v

def low_keep(v):
    return (low(v), None)

def low_pass(kept, grad):
    return (grad,)

def back_keep(v):
    return (v, None)

def back_low(kept, grad):
    return (low(grad),)
low.defvjp(low_keep, low_pass)
low_back.defvjp(back_keep, back_low)
EPSILON = 1e-06
SOFTCAP = 50.0
LEVEL_PULL = 0.75
TWO_PI = 2.0 * math.pi

def matmul(left, right):
    return jnp.dot(left, right, precision=lax.Precision.HIGHEST, preferred_element_type=jnp.float32)

def rms_scale(vector_in, gain_row):
    mean_sq = lax.optimization_barrier(jnp.mean(vector_in * vector_in, axis=-1, keepdims=True))
    return vector_in * lax.rsqrt(mean_sq + EPSILON) * (1.0 + gain_row)

def soft_level(value):
    return value - LEVEL_PULL * jnp.sin(TWO_PI * value) / TWO_PI

def nested(weight, channel_scale):
    scaled_w = weight / channel_scale
    level_eight = soft_level(127.0 * scaled_w)
    level_four = 16.0 * soft_level(level_eight / 16.0)
    level_two = 64.0 * soft_level(level_eight / 64.0)
    return channel_scale * (level_eight + level_four + level_two) / 381.0

def rotate(vector_in, cosine, sine_tab):
    half_dim = vector_in.shape[-1] // 2
    first_half = vector_in[..., :half_dim]
    second_half = vector_in[..., half_dim:]
    return jnp.concatenate([first_half * cosine - second_half * sine_tab, second_half * cosine + first_half * sine_tab], axis=-1)

def rope_tables(position, head_dim):
    half_dim = head_dim // 2
    frequency = jnp.exp(jnp.arange(half_dim, dtype=jnp.float32) * (-2.0 * math.log(10000.0) / head_dim))
    angle = position.astype(jnp.float32)[:, None] * frequency[None, :]
    return (jnp.cos(angle)[:, None, :], jnp.sin(angle)[:, None, :])

def doc_info(lengths, places):
    stop_at = jnp.cumsum(lengths, dtype=jnp.int32)
    starts = stop_at - lengths
    inside = starts[None, :] <= places[:, None]
    doc_index = (lax.optimization_barrier(jnp.sum(inside.astype(jnp.int32), axis=1)) - 1).astype(jnp.int32)
    doc_start = lax.optimization_barrier(jnp.max(jnp.where(inside, starts[None, :], 0), axis=1))
    return (doc_index, places - doc_start)

def glu(gate_in, up_in):
    return jax.nn.gelu(gate_in, approximate=True) * up_in

def attention(queries, key_rows, value_rows, doc_index):
    block_rows = SHARD
    block_count = TOKENS // block_rows
    key_pad = jnp.concatenate([jnp.zeros((WINDOW, KVH, HD), key_rows.dtype), key_rows], axis=0)
    value_pad = jnp.concatenate([jnp.zeros((WINDOW, KVH, HD), value_rows.dtype), value_rows], axis=0)
    docs_pad = jnp.concatenate([jnp.full((WINDOW,), -1, jnp.int32), doc_index], axis=0)
    distance = (WINDOW + jnp.arange(block_rows, dtype=jnp.int32))[:, None] - jnp.arange(WINDOW + block_rows, dtype=jnp.int32)[None, :]
    root = math.sqrt(HD)

    def one_block(block_index):
        first_row = (block_index * block_rows).astype(jnp.int32)
        query_blk = lax.dynamic_slice_in_dim(queries, first_row, block_rows, 0).reshape(block_rows, KVH, G, HD)
        key_blk = lax.dynamic_slice_in_dim(key_pad, first_row, WINDOW + block_rows, 0)
        value_blk = lax.dynamic_slice_in_dim(value_pad, first_row, WINDOW + block_rows, 0)
        q_doc = lax.dynamic_slice_in_dim(doc_index, first_row, block_rows, 0)
        k_doc = lax.dynamic_slice_in_dim(docs_pad, first_row, WINDOW + block_rows, 0)
        allowed = (q_doc[:, None] == k_doc[None, :]) & (distance >= 0) & (distance < WINDOW)
        raw_scores = low_back(jnp.einsum('bhgd,chd->hgbc', query_blk, key_blk, precision=lax.Precision.HIGHEST) / root)
        capped = jnp.where(allowed[None, None], SOFTCAP * jnp.tanh(raw_scores / SOFTCAP), -1e+30)
        row_max = lax.optimization_barrier(jnp.max(capped, axis=3, keepdims=True))
        exp_scores = jnp.exp(capped - row_max)
        attn_probs = low(exp_scores / lax.optimization_barrier(jnp.sum(exp_scores, axis=3, keepdims=True)))
        outputs = jnp.einsum('hgbc,chd->bhgd', attn_probs, value_blk, precision=lax.Precision.HIGHEST)
        return outputs.reshape(block_rows, QH * HD)
    blocks = lax.map(jax.checkpoint(one_block), jnp.arange(block_count, dtype=jnp.int32))
    return blocks.reshape(TOKENS, QH * HD)

def forward(inputs, gains, qkv_e, out_e, in_e, down_e, doc_index, cosine, sine_tab):
    normed = low(rms_scale(inputs, gains[0]))
    mixed_qkv = low_back(matmul(normed, qkv_e))
    grouped = mixed_qkv.reshape(TOKENS, KVH, G + 2, HD)
    queries = low(low_back(rotate(grouped[:, :, :G].reshape(TOKENS, QH, HD), cosine, sine_tab)))
    key_rows = low(low_back(rotate(grouped[:, :, G], cosine, sine_tab)))
    value_rows = low(low_back(grouped[:, :, G + 1]))
    heads = low(low_back(attention(queries, key_rows, value_rows, doc_index)))
    branch = low_back(matmul(heads, out_e.T))
    middle = inputs + rms_scale(branch, gains[1])
    pre_mlp = low(rms_scale(middle, gains[2]))
    mlp_rows = min(TOKENS, 4096)

    def mlp_block(row_block):
        gate_up = low_back(matmul(row_block, in_e))
        hidden = low(glu(gate_up[:, :FF], gate_up[:, FF:]))
        return low_back(matmul(hidden, down_e.T))
    down_out = lax.map(jax.checkpoint(mlp_block), pre_mlp.reshape(TOKENS // mlp_rows, mlp_rows, D)).reshape(TOKENS, D)
    return middle + rms_scale(down_out, gains[3])

def reference(tokens, gains, w_qkv, w_out, w_in, w_down, lengths, cotangent):
    places = jnp.arange(TOKENS, dtype=jnp.int32)
    doc_index, position = doc_info(lengths, places)
    cosine, sine_tab = rope_tables(position, HD)
    qkv_f = w_qkv.astype(jnp.float32)
    out_f = w_out.astype(jnp.float32)
    in_f = w_in.astype(jnp.float32)
    down_f = w_down.astype(jnp.float32)
    qkv_scale = lax.optimization_barrier(jnp.max(jnp.abs(qkv_f), axis=0)) + EPSILON
    in_scale = lax.optimization_barrier(jnp.max(jnp.abs(in_f), axis=0)) + EPSILON
    out_scale = lax.optimization_barrier(jnp.max(jnp.abs(out_f), axis=1)) + EPSILON
    down_scale = lax.optimization_barrier(jnp.max(jnp.abs(down_f), axis=1)) + EPSILON
    qkv_e = low(nested(qkv_f, qkv_scale[None, :]))
    out_e = low(nested(out_f, out_scale[:, None]))
    in_e = low(nested(in_f, in_scale[None, :]))
    down_e = low(nested(down_f, down_scale[:, None]))

    def closed(inputs, gains_f, qkv_w, out_w, in_w, down_w):
        return forward(inputs, gains_f, qkv_w, out_w, in_w, down_w, doc_index, cosine, sine_tab)
    primal, pullback = jax.vjp(closed, tokens.astype(jnp.float32), gains, qkv_e, out_e, in_e, down_e)
    grad_list = pullback(cotangent.astype(jnp.float32))
    column_scales = jnp.concatenate([qkv_scale, in_scale], axis=0)
    row_scales = jnp.stack([out_scale, down_scale], axis=0)
    return (primal.astype(jnp.bfloat16), grad_list[0], grad_list[2], grad_list[3], grad_list[4], grad_list[5], grad_list[1], column_scales, row_scales)
```

```python
import math

import jax
import jax.numpy as jnp
import numpy as np
from jax import lax
from jax.sharding import Mesh
from jax.sharding import PartitionSpec as P

FF = 9216
QH = 8
KVH = 4
HD = 256
WINDOW = 4096

EPSILON = 1e-06
SOFTCAP = 50.0
LEVEL_PULL = 0.75
TWO_PI = 2.0 * math.pi

FINE = ("zh", "zl", "x", "y", "c")
LINE = ("zh", "zl")
PLANE = ("x", "y", "c")
CUBE = ("zl", "x", "y")
SWAP = ((0, 1), (1, 0))

SINE = (
    25.13274115538592,
    -64.83582285607088,
    67.07662736368954,
    -38.49587868201696,
    14.049662842567686,
    -3.16160028673954,
)

f32 = jnp.float32
bf16 = jnp.bfloat16


def sin_turns(turns):
    part = turns - jnp.round(turns)
    square = part * part
    poly = SINE[5]
    for factor in SINE[4::-1]:
        poly = poly * square + factor
    return part * (0.25 - square) * poly


def rms_scale(vector_in, gain_row):
    mean_sq = jnp.mean(vector_in * vector_in, axis=-1, keepdims=True)
    return vector_in * lax.rsqrt(mean_sq + EPSILON) * (1.0 + gain_row)


def nested(weight, channel_scale):
    level = weight * (127.0 / channel_scale)
    level = level - (LEVEL_PULL / TWO_PI) * sin_turns(level)
    four = sin_turns(level * (1.0 / 16.0))
    two = sin_turns(level * (1.0 / 64.0))
    total = 3.0 * level - (16.0 * LEVEL_PULL / TWO_PI) * four - (64.0 * LEVEL_PULL / TWO_PI) * two
    return (channel_scale / 381.0) * total


def rotate(vector_in, cosine, sine_tab):
    half_dim = vector_in.shape[-1] // 2
    first_half = vector_in[..., :half_dim]
    second_half = vector_in[..., half_dim:]
    return jnp.concatenate(
        [
            first_half * cosine - second_half * sine_tab,
            second_half * cosine + first_half * sine_tab,
        ],
        axis=-1,
    )


def rope_tables(position, head_dim):
    half_dim = head_dim // 2
    frequency = np.exp(np.arange(half_dim) * (-2.0 * math.log(10000.0) / head_dim)) / TWO_PI
    coarse = frequency.astype(jnp.bfloat16).astype(np.float32)
    fine = (frequency - coarse).astype(np.float32)
    place = position.astype(f32)[:, None]
    turns = place * coarse[None, :]
    turns = (turns - jnp.round(turns)) + place * fine[None, :]
    return (sin_turns(turns + 0.25), sin_turns(turns))


def doc_info(lengths, places):
    stop_at = jnp.cumsum(lengths, dtype=jnp.int32)
    starts = stop_at - lengths
    inside = starts[None, :] <= places[:, None]
    doc_index = jnp.sum(inside.astype(jnp.int32), axis=1) - 1
    doc_start = jnp.max(jnp.where(inside, starts[None, :], 0), axis=1)
    return (doc_index, places - doc_start)


def glu(gate_in, up_in):
    return jax.nn.gelu(gate_in, approximate=True) * up_in


def dot(left, right, dims, out=f32):
    return lax.dot_general(left, right, (dims, ((), ())), preferred_element_type=out)


ROWS = ((1,), (1,))
COLS = ((1,), (0,))
FIRST = ((0,), (0,))


def swap(value, axis):
    return lax.ppermute(value, axis, SWAP)


def gather_blocks(block, axes, orders):
    rows, width = block.shape
    part = width // len(orders)
    parts = []
    for i, order in enumerate(orders):
        held = block[:, i * part : (i + 1) * part].reshape((1,) * len(axes) + (rows, part))
        for axis in order:
            held = jnp.concatenate([held, swap(held, axis)], axis=axes.index(axis))
        parts.append(held)
    return jnp.concatenate(parts, axis=-1).reshape(-1, width)


def scatter_blocks(partial, axes, orders):
    width = partial.shape[-1]
    part = width // len(orders)
    blocks = partial.reshape((2,) * len(axes) + (-1, width))
    parts = []
    for i, order in enumerate(orders):
        held = blocks[..., i * part : (i + 1) * part]
        for axis in order:
            at = axes.index(axis)
            keep = lax.slice_in_dim(held, 0, 1, axis=at)
            send = lax.slice_in_dim(held, 1, 2, axis=at).astype(bf16)
            held = keep.astype(f32) + swap(send, axis).astype(f32)
        parts.append(held.reshape(-1, part))
    return jnp.concatenate(parts, axis=-1)


TOKEN_AXES = ("c", "x", "y")
PLANE_GATHER = (("x", "y", "c"), ("y", "x", "c"))
PLANE_SCATTER = (("c", "y", "x"), ("c", "x", "y"))
CUBE_GATHER = (("zl", "x", "y"), ("x", "y", "zl"), ("y", "zl", "x"))
CUBE_SCATTER = (("y", "x", "zl"), ("zl", "y", "x"), ("x", "zl", "y"))


def both(value, axis):
    if lax.axis_size(axis) != 2:
        return lax.all_gather(value, axis, axis=0)
    other = swap(value, axis)
    first = lax.axis_index(axis) == 0
    return jnp.stack([jnp.where(first, value, other), jnp.where(first, other, value)], axis=0)


def sum_both(value, axis, dim):
    if lax.axis_size(axis) != 2:
        moved = jnp.moveaxis(value, dim, 0)
        return lax.psum_scatter(moved.astype(bf16), axis, scatter_dimension=0, tiled=False)
    me = lax.axis_index(axis)
    send = lax.dynamic_index_in_dim(value, 1 - me, dim, keepdims=False).astype(bf16)
    keep = lax.dynamic_index_in_dim(value, me, dim, keepdims=False)
    return (keep.astype(f32) + swap(send, axis).astype(f32)).astype(bf16)


def max_both(value, axis):
    if lax.axis_size(axis) != 2:
        return lax.pmax(value, axis)
    return jnp.maximum(value, swap(value, axis))


def widen(part):
    cube, own, width = part.shape
    line = both(part, "zh")
    full = both(line, "c")
    return full.transpose(1, 2, 0, 3, 4).reshape(-1, width)


def narrow(grad, own):
    width = grad.shape[-1]
    split = grad.reshape(lax.axis_size("zh"), 8, 2, own, width)
    mine = sum_both(split, "c", 2)
    return sum_both(mine, "zh", 0)


def exchange(value, axes):
    return lax.all_to_all(value, axes, split_axis=0, concat_axis=0, tiled=True)


def on_device(tokens, gains, w_qkv, w_out, w_in, w_down, lengths, cotangent):
    line_count = lax.axis_size(LINE)
    line_index = lax.axis_index(LINE)
    core = lax.axis_index("c")
    x_index = lax.axis_index("x")
    y_index = lax.axis_index("y")
    tok_rows, model = tokens.shape
    own = w_qkv.shape[0]
    block_rows = 8 * tok_rows
    total_rows = line_count * block_rows
    root = math.sqrt(HD)
    slice_ff = FF // 8

    qkv_out = w_qkv.reshape(own, KVH, 2, 2, HD).transpose(1, 3, 0, 2, 4).reshape(8, own, 2 * HD)
    qkv_out = jnp.broadcast_to(qkv_out[None], (line_count, 8, own, 2 * HD))
    qkv_lat = exchange(qkv_out.reshape(line_count * 8, own, 2 * HD), FINE).reshape(model, 2 * HD)

    inputs = tokens.astype(f32)
    normed = rms_scale(inputs, gains[0]).astype(bf16)
    normed_all = gather_blocks(normed, TOKEN_AXES, PLANE_GATHER)

    in_lat = exchange(
        w_in.reshape(own, 2, 8, slice_ff).transpose(2, 0, 1, 3).reshape(8, own, 2 * slice_ff), CUBE
    )

    out_scale = jnp.max(jnp.abs(w_out.astype(f32)), axis=1) + EPSILON
    down_scale = jnp.max(jnp.abs(w_down.astype(f32)), axis=1) + EPSILON
    eff_out = nested(w_out.astype(f32), out_scale[:, None]).astype(bf16)
    eff_out = eff_out.reshape(own, 8, HD).transpose(1, 0, 2)
    eff_out = jnp.broadcast_to(eff_out[None], (line_count, 8, own, HD))
    head_out = exchange(eff_out.reshape(line_count * 8, own, HD), FINE).reshape(model, HD)

    eff_down = nested(w_down.astype(f32), down_scale[:, None]).astype(bf16)
    eff_down = exchange(eff_down.reshape(own, 8, slice_ff).transpose(1, 0, 2), CUBE)

    qkv_max = jnp.max(jnp.abs(qkv_lat), axis=0)
    qkv_scale = qkv_max.astype(f32) + EPSILON
    head_qkv = nested(qkv_lat.astype(f32), qkv_scale[None, :]).astype(bf16)

    in_max = max_both(max_both(jnp.max(jnp.abs(in_lat), axis=(0, 1)), "c"), "zh")
    in_scale = in_max.astype(f32) + EPSILON
    cols_in = widen(nested(in_lat.astype(f32), in_scale[None, None, :]).astype(bf16))
    cols_down = widen(eff_down)

    dev = jnp.arange(8, dtype=jnp.int32)
    dev = (
        ((dev // 2 % 2) ^ x_index) * 4 + ((dev % 2) ^ y_index) * 2 + ((dev // 4) ^ core)
    ).astype(jnp.int32)
    inner = (dev[:, None] * tok_rows + jnp.arange(tok_rows, dtype=jnp.int32)[None, :]).reshape(-1)
    q_places = line_index * block_rows + inner
    q_doc, position = doc_info(lengths, q_places)
    cosine, sine_tab = rope_tables(position, HD)

    mixed = dot(normed_all, head_qkv, COLS)
    query = rotate(mixed[:, :HD], cosine, sine_tab).astype(bf16)
    second = mixed[:, HD:]
    kv_own = jnp.where(core == 0, rotate(second, cosine, sine_tab), second).astype(bf16)

    reach = min(WINDOW, total_rows // 2)
    back = min(line_count - 1, -(-(reach - 1) // block_rows))
    shifted = [kv_own]
    for n in range(1, back + 1):
        shifted.append(
            lax.ppermute(kv_own, LINE, [(i, i + n) for i in range(line_count - n)])
        )
    kv_mine = jnp.stack(shifted[::-1], axis=0)
    kv_flip = swap(kv_mine, "c")
    half_block = block_rows // 2
    kv_flip = jnp.concatenate([kv_flip[:, half_block:], kv_flip[:, :half_block]], axis=1)
    key_rows = jnp.where(core == 0, kv_mine, kv_flip).reshape(-1, HD)
    value_rows = jnp.where(core == 0, kv_flip, kv_mine).reshape(-1, HD)
    k_places = jnp.concatenate(
        [q_places - n * block_rows for n in range(back, -1, -1)], axis=0
    )
    k_doc = doc_info(lengths, k_places)[0]
    distance = q_places[:, None] - k_places[None, :]
    allowed = (q_doc[:, None] == k_doc[None, :]) & (distance >= 0) & (distance < WINDOW)

    tanh_part = jnp.tanh(dot(query, key_rows, ROWS) * (1.0 / (root * SOFTCAP)))
    capped = jnp.where(allowed, SOFTCAP * tanh_part, -1e30)
    row_max = jnp.max(capped, axis=1, keepdims=True)
    exp_scores = jnp.exp(capped - row_max)
    row_total = jnp.sum(exp_scores, axis=1, keepdims=True)
    probs = exp_scores / row_total
    probs_low = probs.astype(bf16)
    heads = dot(probs_low, value_rows, COLS).astype(bf16)

    branch = scatter_blocks(dot(heads, head_out, ROWS, bf16), TOKEN_AXES, PLANE_SCATTER)
    middle = inputs + rms_scale(branch, gains[1])
    pre_mlp = rms_scale(middle, gains[2]).astype(bf16)

    pre_all = gather_blocks(pre_mlp, CUBE, CUBE_GATHER)
    gate_up = dot(pre_all, cols_in, COLS)
    gate_part = gate_up[:, :slice_ff]
    up_part = gate_up[:, slice_ff:]
    hidden = glu(gate_part, up_part).astype(bf16)
    down_out = scatter_blocks(dot(hidden, cols_down, ROWS, bf16), CUBE, CUBE_SCATTER)
    result = (middle + rms_scale(down_out, gains[3])).astype(bf16)

    grad_result = cotangent.astype(f32)
    d_down, gain_four = jax.vjp(rms_scale, down_out, gains[3])[1](grad_result)
    d_down = d_down.astype(bf16)
    d_down_all = gather_blocks(d_down, CUBE, CUBE_GATHER)
    part_down = dot(d_down_all, hidden, FIRST, bf16)
    d_hidden = dot(d_down_all, cols_down, COLS)
    d_gate, d_up = jax.vjp(glu, gate_part, up_part)[1](d_hidden)
    d_both = jnp.concatenate([d_gate, d_up], axis=1).astype(bf16)
    d_pre = scatter_blocks(dot(d_both, cols_in, ROWS, bf16), CUBE, CUBE_SCATTER)
    part_in = dot(pre_all, d_both, FIRST, bf16)

    grad_down = exchange(narrow(part_down, own), CUBE)
    grad_down = grad_down.transpose(1, 0, 2).reshape(own, FF).astype(f32)
    grad_in = exchange(narrow(part_in, own), CUBE)
    grad_in = grad_in.reshape(8, own, 2, slice_ff).transpose(1, 2, 0, 3)
    grad_in = grad_in.reshape(own, 2 * FF).astype(f32)

    d_mid_part, gain_three = jax.vjp(rms_scale, middle, gains[2])[1](d_pre)
    d_middle = grad_result + d_mid_part
    d_branch, gain_two = jax.vjp(rms_scale, branch, gains[1])[1](d_middle)
    d_branch_all = gather_blocks(d_branch.astype(bf16), TOKEN_AXES, PLANE_GATHER)
    d_heads = dot(d_branch_all, head_out, COLS).astype(bf16)
    part_out = dot(d_branch_all, heads, FIRST, bf16)
    grad_out = exchange(part_out.reshape(line_count * 8, own, HD), FINE)
    grad_out = jnp.sum(grad_out.reshape(line_count, 8, own, HD).astype(f32), axis=0)
    grad_out = grad_out.transpose(1, 0, 2).reshape(own, QH * HD)

    d_prob = dot(d_heads, value_rows, ROWS)
    delta = jnp.sum(probs * d_prob, axis=1, keepdims=True)
    d_raw = (probs * (d_prob - delta) * (1.0 - tanh_part * tanh_part)).astype(bf16)
    d_query = (dot(d_raw, key_rows, COLS) * (1.0 / root)).astype(bf16)
    d_keys = dot(d_raw, query, FIRST) * (1.0 / root)
    d_values = dot(probs_low, d_heads, FIRST)
    d_keys = d_keys.reshape(back + 1, block_rows, HD)
    d_values = d_values.reshape(back + 1, block_rows, HD)
    send = jnp.where(core == 0, d_values, d_keys).astype(bf16)
    send = jnp.concatenate([send[:, half_block:], send[:, :half_block]], axis=1)
    d_window = jnp.where(core == 0, d_keys, d_values) + swap(send, "c").astype(f32)
    d_kv = d_window[back]
    for n in range(1, back + 1):
        d_kv = d_kv + lax.ppermute(
            d_window[back - n].astype(bf16), LINE, [(i + n, i) for i in range(line_count - n)]
        ).astype(f32)
    d_kv = d_kv.astype(bf16).astype(f32)
    d_query_lin = rotate(d_query.astype(f32), cosine, -sine_tab)
    d_second = jnp.where(core == 0, rotate(d_kv, cosine, -sine_tab), d_kv)
    d_mixed = jnp.concatenate([d_query_lin, d_second], axis=1).astype(bf16)

    d_normed = scatter_blocks(dot(d_mixed, head_qkv, ROWS, bf16), TOKEN_AXES, PLANE_SCATTER)
    d_input_part, gain_one = jax.vjp(rms_scale, inputs, gains[0])[1](d_normed)
    grad_tokens = d_middle + d_input_part
    part_qkv = dot(normed_all, d_mixed, FIRST, bf16)
    grad_qkv = exchange(part_qkv.reshape(line_count * 8, own, 2 * HD), FINE)
    grad_qkv = jnp.sum(grad_qkv.reshape(line_count, 8, own, 2 * HD).astype(f32), axis=0)
    grad_qkv = grad_qkv.reshape(KVH, 2, own, 2, HD).transpose(2, 0, 3, 1, 4)
    grad_qkv = grad_qkv.reshape(own, KVH * 4 * HD)

    grad_gains = lax.psum(jnp.stack([gain_one, gain_two, gain_three, gain_four], axis=0), FINE)
    qkv_scales = lax.all_gather(qkv_scale, PLANE, axis=0).reshape(KVH, 2, 2, HD)
    qkv_scales = qkv_scales.transpose(0, 2, 1, 3).reshape(-1)
    in_scales = lax.all_gather(in_scale, CUBE, axis=0).reshape(8, 2, slice_ff)
    in_scales = in_scales.transpose(1, 0, 2).reshape(-1)
    column_scales = jnp.concatenate([qkv_scales, in_scales], axis=0)
    row_scales = jnp.stack([out_scale, down_scale], axis=0)
    return (
        result,
        grad_tokens,
        grad_qkv,
        grad_out,
        grad_in,
        grad_down,
        grad_gains,
        column_scales,
        row_scales,
    )


def solution(mesh):
    fine = Mesh(
        mesh.devices.reshape(mesh.shape["sp"] // 4, 2, 2, mesh.shape["hd"] // 2, 2), FINE
    )
    split = P(FINE, None)
    in_specs = (split, P(), split, split, split, split, P(), split)
    out_specs = (split, split, split, split, split, split, P(), P(), P(None, FINE))
    return jax.shard_map(
        on_device, mesh=fine, in_specs=in_specs, out_specs=out_specs, check_vma=False
    )
```

```python
import math

import jax
import jax.numpy as jnp
import numpy as np
from jax import lax
from jax.experimental import pallas as pl
from jax.experimental.pallas import tpu as pltpu
from jax.sharding import Mesh
from jax.sharding import PartitionSpec as P

FF = 9216
QH = 8
KVH = 4
HD = 256
WINDOW = 4096

EPSILON = 1e-06
SOFTCAP = 50.0
LEVEL_PULL = 0.75
TWO_PI = 2.0 * math.pi

FINE = ("zh", "zl", "x", "y", "c")
LINE = ("zh", "zl")
PLANE = ("x", "y", "c")
CUBE = ("zl", "x", "y")
SWAP = ((0, 1), (1, 0))

SINE = (
    25.13274115538592,
    -64.83582285607088,
    67.07662736368954,
    -38.49587868201696,
    14.049662842567686,
    -3.16160028673954,
)

f32 = jnp.float32
bf16 = jnp.bfloat16


def sin_turns(turns):
    part = turns - jnp.round(turns)
    square = part * part
    poly = SINE[5]
    for factor in SINE[4::-1]:
        poly = poly * square + factor
    return part * (0.25 - square) * poly


def rms_scale(vector_in, gain_row):
    mean_sq = jnp.mean(vector_in * vector_in, axis=-1, keepdims=True)
    return vector_in * lax.rsqrt(mean_sq + EPSILON) * (1.0 + gain_row)


def nested(weight, channel_scale):
    level = weight * (127.0 / channel_scale)
    level = level - (LEVEL_PULL / TWO_PI) * sin_turns(level)
    four = sin_turns(level * (1.0 / 16.0))
    two = sin_turns(level * (1.0 / 64.0))
    total = 3.0 * level - (16.0 * LEVEL_PULL / TWO_PI) * four - (64.0 * LEVEL_PULL / TWO_PI) * two
    return (channel_scale / 381.0) * total


def rotate(vector_in, cosine, sine_tab):
    half_dim = vector_in.shape[-1] // 2
    first_half = vector_in[..., :half_dim]
    second_half = vector_in[..., half_dim:]
    return jnp.concatenate(
        [
            first_half * cosine - second_half * sine_tab,
            second_half * cosine + first_half * sine_tab,
        ],
        axis=-1,
    )


def rope_tables(position, head_dim):
    half_dim = head_dim // 2
    frequency = np.exp(np.arange(half_dim) * (-2.0 * math.log(10000.0) / head_dim)) / TWO_PI
    coarse = frequency.astype(jnp.bfloat16).astype(np.float32)
    fine = (frequency - coarse).astype(np.float32)
    place = position.astype(f32)[:, None]
    turns = place * coarse[None, :]
    turns = (turns - jnp.round(turns)) + place * fine[None, :]
    return (sin_turns(turns + 0.25), sin_turns(turns))


def doc_info(lengths, places):
    stop_at = jnp.cumsum(lengths, dtype=jnp.int32)
    starts = stop_at - lengths
    inside = starts[None, :] <= places[:, None]
    doc_index = jnp.sum(inside.astype(jnp.int32), axis=1) - 1
    doc_start = jnp.max(jnp.where(inside, starts[None, :], 0), axis=1)
    return (doc_index, places - doc_start)


def glu(gate_in, up_in):
    return jax.nn.gelu(gate_in, approximate=True) * up_in


def dot(left, right, dims, out=f32):
    return lax.dot_general(left, right, (dims, ((), ())), preferred_element_type=out)


ROWS = ((1,), (1,))
COLS = ((1,), (0,))
FIRST = ((0,), (0,))


def swap(value, axis):
    return lax.ppermute(value, axis, SWAP)


def gather_blocks(block, axes, orders):
    rows, width = block.shape
    part = width // len(orders)
    parts = []
    for i, order in enumerate(orders):
        held = block[:, i * part : (i + 1) * part].reshape((1,) * len(axes) + (rows, part))
        for axis in order:
            held = jnp.concatenate([held, swap(held, axis)], axis=axes.index(axis))
        parts.append(held)
    return jnp.concatenate(parts, axis=-1).reshape(-1, width)


def scatter_blocks(partial, axes, orders):
    width = partial.shape[-1]
    part = width // len(orders)
    blocks = partial.reshape((2,) * len(axes) + (-1, width))
    parts = []
    for i, order in enumerate(orders):
        held = blocks[..., i * part : (i + 1) * part]
        for axis in order:
            at = axes.index(axis)
            keep = lax.slice_in_dim(held, 0, 1, axis=at)
            send = lax.slice_in_dim(held, 1, 2, axis=at).astype(bf16)
            held = keep.astype(f32) + swap(send, axis).astype(f32)
        parts.append(held.reshape(-1, part))
    return jnp.concatenate(parts, axis=-1)


TOKEN_AXES = ("c", "x", "y")
PLANE_GATHER = (("x", "y", "c"), ("y", "x", "c"))
PLANE_SCATTER = (("c", "y", "x"), ("c", "x", "y"))
CUBE_GATHER = (("zl", "x", "y"), ("x", "y", "zl"), ("y", "zl", "x"))
CUBE_SCATTER = (("y", "x", "zl"), ("zl", "y", "x"), ("x", "zl", "y"))


def after(value, *events):
    return lax.optimization_barrier((value,) + events)[0]


def both(value, axis):
    other = swap(value, axis)
    first = lax.axis_index(axis) == 0
    return jnp.stack([jnp.where(first, value, other), jnp.where(first, other, value)], axis=0)


def core_sum(grad, own):
    split = grad.reshape(lax.axis_size("zh"), 8, 2, own, grad.shape[-1])
    me = lax.axis_index("c")
    send = lax.dynamic_index_in_dim(split, 1 - me, 2, keepdims=False)
    keep = lax.dynamic_index_in_dim(split, me, 2, keepdims=False)
    return (keep.astype(f32) + swap(send, "c").astype(f32)).astype(bf16)


def line_sum(part):
    flat = part.reshape(-1, part.shape[-1])
    return lax.psum_scatter(flat, "zh", scatter_dimension=0, tiled=True).reshape(part.shape[1:])


def max_both(value, axis):
    return jnp.maximum(value, swap(value, axis))


def sum_all(value):
    for axis in ("c", "x", "y", "zl", "zh"):
        if lax.axis_size(axis) == 2:
            value = value + swap(value, axis)
        else:
            value = lax.psum(value, axis)
    return value


def shift(value, step):
    count = lax.axis_size(LINE)
    return lax.ppermute(value, LINE, [(i, i + step) for i in range(count) if 0 <= i + step < count])


def by_core(part):
    other = swap(part, "c")
    full = jnp.broadcast_to(part[:, :, None], part.shape[:2] + (2,) + part.shape[2:])
    full = lax.dynamic_update_slice_in_dim(full, other[:, :, None], 1 - lax.axis_index("c"), 2)
    return full.reshape(-1, part.shape[-1])


Q_ROWS = 128


def scores(q_ref, k_ref, low_ref, place_ref, k_place_ref):
    raw = dot(q_ref[...], k_ref[...], ROWS) * (1.0 / (math.sqrt(HD) * SOFTCAP))
    places = k_place_ref[...]
    allowed = (places >= low_ref[...]) & (places <= place_ref[...])
    return jnp.tanh(raw), allowed


def attend_kernel(q_ref, k_ref, v_ref, low_ref, place_ref, k_place_ref, out_ref, lse_ref):
    tanh_part, allowed = scores(q_ref, k_ref, low_ref, place_ref, k_place_ref)
    capped = jnp.where(allowed, SOFTCAP * tanh_part, -1e30)
    row_max = jnp.max(capped, axis=1, keepdims=True)
    exp_scores = jnp.exp(capped - row_max)
    row_total = jnp.sum(exp_scores, axis=1, keepdims=True)
    probs = (exp_scores * (1.0 / row_total)).astype(bf16)
    out_ref[...] = dot(probs, v_ref[...], COLS).astype(bf16)
    lse_ref[...] = row_max + jnp.log(row_total)


def attend_back_kernel(
    q_ref, k_ref, v_ref, low_ref, place_ref, k_place_ref, lse_ref, d_ref, dq_ref, dk_ref, dv_ref
):
    @pl.when(pl.program_id(0) == 0)
    def _():
        dk_ref[...] = jnp.zeros_like(dk_ref)
        dv_ref[...] = jnp.zeros_like(dv_ref)

    scale = 1.0 / math.sqrt(HD)
    tanh_part, allowed = scores(q_ref, k_ref, low_ref, place_ref, k_place_ref)
    probs = jnp.where(allowed, jnp.exp(SOFTCAP * tanh_part - lse_ref[...]), 0.0)
    dv_ref[...] += dot(probs.astype(bf16), d_ref[...], FIRST)
    d_prob = dot(d_ref[...], v_ref[...], ROWS)
    delta = jnp.sum(probs * d_prob, axis=1, keepdims=True)
    d_raw = (probs * (d_prob - delta) * (1.0 - tanh_part * tanh_part)).astype(bf16)
    dq_ref[...] = (dot(d_raw, k_ref[...], COLS) * scale).astype(bf16)
    dk_ref[...] += dot(d_raw, q_ref[...], FIRST) * scale


def attention_specs(rows, keys):
    q_spec = pl.BlockSpec((Q_ROWS, HD), lambda i: (i, 0))
    k_spec = pl.BlockSpec((keys, HD), lambda i: (0, 0))
    row_spec = pl.BlockSpec((Q_ROWS, 1), lambda i: (i, 0))
    place_spec = pl.BlockSpec((1, keys), lambda i: (0, 0))
    common = dict(
        grid=(rows // Q_ROWS,),
        compiler_params=pltpu.CompilerParams(
            dimension_semantics=("arbitrary",), vmem_limit_bytes=56 * 2**20
        ),
        cost_estimate=pl.CostEstimate(flops=1, bytes_accessed=1, transcendentals=0),
    )
    return q_spec, k_spec, row_spec, place_spec, common


def attend(query, key_rows, value_rows, low, place, k_place):
    rows, keys = query.shape[0], key_rows.shape[0]
    q_spec, k_spec, row_spec, place_spec, common = attention_specs(rows, keys)
    return pl.pallas_call(
        attend_kernel,
        out_shape=(
            jax.ShapeDtypeStruct((rows, HD), bf16),
            jax.ShapeDtypeStruct((rows, 1), f32),
        ),
        in_specs=[q_spec, k_spec, k_spec, row_spec, row_spec, place_spec],
        out_specs=(q_spec, row_spec),
        **common,
    )(query, key_rows, value_rows, low, place, k_place)


def attend_back(query, key_rows, value_rows, low, place, k_place, lse, d_heads):
    rows, keys = query.shape[0], key_rows.shape[0]
    q_spec, k_spec, row_spec, place_spec, common = attention_specs(rows, keys)
    return pl.pallas_call(
        attend_back_kernel,
        out_shape=(
            jax.ShapeDtypeStruct((rows, HD), bf16),
            jax.ShapeDtypeStruct((keys, HD), f32),
            jax.ShapeDtypeStruct((keys, HD), f32),
        ),
        in_specs=[q_spec, k_spec, k_spec, row_spec, row_spec, place_spec, row_spec, q_spec],
        out_specs=(q_spec, k_spec, k_spec),
        **common,
    )(query, key_rows, value_rows, low, place, k_place, lse, d_heads)


def exchange(value, axes):
    return lax.all_to_all(value, axes, split_axis=0, concat_axis=0, tiled=True)


def columns(weight, count):
    own, width = weight.shape
    return weight.reshape(own, count, width // count).transpose(1, 0, 2)


def uncolumns(parts):
    count, own, width = parts.shape
    return parts.transpose(1, 0, 2).reshape(own, count * width)


def on_device(tokens, gains, w_qkv, w_out, w_in, w_down, lengths, cotangent):
    line_count = lax.axis_size(LINE)
    line_index = lax.axis_index(LINE)
    core = lax.axis_index("c")
    x_index = lax.axis_index("x")
    y_index = lax.axis_index("y")
    tok_rows, model = tokens.shape
    own = w_qkv.shape[0]
    block_rows = 8 * tok_rows
    total_rows = line_count * block_rows
    slice_ff = FF // 8

    units = lax.optimization_barrier(columns(w_qkv, 16)).reshape(KVH, 2, 2, own, HD)
    qkv_out = units.transpose(0, 2, 1, 3, 4).reshape(8, 2, own, HD)
    qkv_out = jnp.broadcast_to(qkv_out[None], (line_count, 8, 2, own, HD))
    qkv_lat = exchange(qkv_out.reshape(line_count * 8, 2, own, HD), FINE)
    qkv_lat = qkv_lat.reshape(line_count, 8, 2, own, HD)

    inputs = tokens.astype(f32)
    normed = rms_scale(inputs, gains[0]).astype(bf16)
    normed_all = gather_blocks(normed, TOKEN_AXES, PLANE_GATHER)

    out_scale = jnp.max(jnp.abs(w_out.astype(f32)), axis=1) + EPSILON
    down_scale = jnp.max(jnp.abs(w_down.astype(f32)), axis=1) + EPSILON
    eff_out = nested(w_out.astype(f32), out_scale[:, None]).astype(bf16)
    eff_down = nested(w_down.astype(f32), down_scale[:, None]).astype(bf16)
    in_out = lax.optimization_barrier(columns(w_in, 16)).reshape(2, 8, own, slice_ff)
    in_own = exchange(after(in_out.transpose(1, 0, 2, 3), qkv_lat), CUBE)
    in_lat = lax.all_gather(in_own.transpose(1, 0, 2, 3), "zh", axis=0)
    down_own = exchange(after(columns(eff_down, 8), in_own), CUBE)
    down_lat = lax.all_gather(after(down_own, in_lat), "zh", axis=0)
    eff_out = jnp.broadcast_to(columns(eff_out, 8)[None], (line_count, 8, own, HD))
    head_out = exchange(after(eff_out.reshape(line_count * 8, own, HD), down_own), FINE)
    head_out = head_out.reshape(model, HD)

    qkv_max = jnp.max(jnp.abs(qkv_lat), axis=(0, 1, 3))
    qkv_scale = qkv_max.astype(f32) + EPSILON
    head_qkv = nested(qkv_lat.astype(f32), qkv_scale[None, None, :, None, :]).astype(bf16)
    head_q = head_qkv[:, :, 0].reshape(model, HD)
    head_kv = head_qkv[:, :, 1].reshape(model, HD)

    dev = jnp.arange(8, dtype=jnp.int32)
    dev = (
        ((dev // 2 % 2) ^ x_index) * 4 + ((dev % 2) ^ y_index) * 2 + ((dev // 4) ^ core)
    ).astype(jnp.int32)
    inner = (dev[:, None] * tok_rows + jnp.arange(tok_rows, dtype=jnp.int32)[None, :]).reshape(-1)
    q_places = line_index * block_rows + inner
    position = doc_info(lengths, q_places)[1]
    cosine, sine_tab = rope_tables(position, HD)

    second = dot(normed_all, head_kv, COLS)
    kv_own = jnp.where(core == 0, rotate(second, cosine, sine_tab), second).astype(bf16)

    reach = min(WINDOW, total_rows // 2)
    back = min(line_count - 1, -(-(reach - 1) // block_rows))
    shifted = [kv_own]
    for _ in range(back):
        shifted.append(shift(shifted[-1], 1))
    query = rotate(dot(normed_all, head_q, COLS), cosine, sine_tab).astype(bf16)

    def effective(lat):
        top = max_both(jnp.max(jnp.abs(lat), axis=(0, 1, 2)), "c")
        scale = top.astype(f32) + EPSILON
        return top, by_core(nested(lat.astype(f32), scale).astype(bf16))

    gate_top, cols_gate = effective(in_lat[:, 0])
    up_top, cols_up = effective(in_lat[:, 1])
    cols_down = by_core(down_lat)

    kv_mine = jnp.stack(shifted[::-1], axis=0)
    kv_flip = swap(kv_mine, "c")
    half_block = block_rows // 2
    kv_flip = jnp.concatenate([kv_flip[:, half_block:], kv_flip[:, :half_block]], axis=1)
    key_rows = jnp.where(core == 0, kv_mine, kv_flip).reshape(-1, HD)
    value_rows = jnp.where(core == 0, kv_flip, kv_mine).reshape(-1, HD)
    k_places = jnp.concatenate(
        [q_places - n * block_rows for n in range(back, -1, -1)], axis=0
    )
    place = q_places[:, None]
    low = jnp.maximum(q_places - position, q_places - (WINDOW - 1))[:, None]
    heads, lse = attend(query, key_rows, value_rows, low, place, k_places[None])

    branch = dot(after(heads, in_lat), head_out, ROWS, bf16)
    branch = scatter_blocks(branch, TOKEN_AXES, PLANE_SCATTER)
    middle = inputs + rms_scale(branch, gains[1])
    pre_mlp = rms_scale(middle, gains[2]).astype(bf16)

    pre_all = gather_blocks(pre_mlp, CUBE, CUBE_GATHER)
    gate_part = dot(pre_all, cols_gate, COLS)
    up_part = dot(pre_all, cols_up, COLS)
    hidden = glu(gate_part, up_part).astype(bf16)
    down_out = scatter_blocks(dot(hidden, cols_down, ROWS, bf16), CUBE, CUBE_SCATTER)
    result = (middle + rms_scale(down_out, gains[3])).astype(bf16)

    grad_result = cotangent.astype(f32)
    d_down, gain_four = jax.vjp(rms_scale, down_out, gains[3])[1](grad_result)
    d_down = d_down.astype(bf16)
    tops = [both(qkv_max.reshape(-1), "c").reshape(-1), gate_top, up_top]
    tops = after(jnp.concatenate(tops, axis=0), d_down)
    tops = both(both(both(tops, "y"), "x"), "zl")
    d_down_all = gather_blocks(d_down, CUBE, CUBE_GATHER)
    d_hidden = dot(after(d_down_all, tops), cols_down, COLS)
    d_gate, d_up = jax.vjp(glu, gate_part, up_part)[1](d_hidden)
    d_gate = d_gate.astype(bf16)
    d_up = d_up.astype(bf16)
    d_pre = (dot(d_gate, cols_gate, ROWS) + dot(d_up, cols_up, ROWS)).astype(bf16)
    part_down = core_sum(dot(d_down_all, hidden, FIRST, bf16), own)
    d_pre = after(d_pre, part_down)
    grad_down = exchange(line_sum(part_down), CUBE)
    part_gate = core_sum(dot(pre_all, after(d_gate, d_pre), FIRST, bf16), own)
    part_up = core_sum(dot(pre_all, after(d_up, d_pre), FIRST, bf16), own)
    part_in = jnp.stack([part_gate, part_up], axis=1)
    d_pre = after(scatter_blocks(d_pre, CUBE, CUBE_SCATTER), part_in)
    part_in = line_sum(part_in).transpose(1, 0, 2, 3)

    d_mid_part, gain_three = jax.vjp(rms_scale, middle, gains[2])[1](d_pre)
    d_middle = grad_result + d_mid_part
    d_branch, gain_two = jax.vjp(rms_scale, branch, gains[1])[1](d_middle)
    d_branch_all = gather_blocks(d_branch.astype(bf16), TOKEN_AXES, PLANE_GATHER)
    d_heads = dot(d_branch_all, head_out, COLS).astype(bf16)

    d_query, d_keys, d_values = attend_back(
        query, key_rows, value_rows, low, place, k_places[None], lse, d_heads
    )
    d_keys = d_keys.reshape(back + 1, block_rows, HD)
    d_values = d_values.reshape(back + 1, block_rows, HD)
    send = jnp.where(core == 0, d_values, d_keys).astype(bf16)
    send = jnp.concatenate([send[:, half_block:], send[:, :half_block]], axis=1)
    d_window = jnp.where(core == 0, d_keys, d_values) + swap(send, "c").astype(f32)
    d_kv = d_window[0]
    for n in range(1, back + 1):
        d_kv = d_window[n] + shift(d_kv.astype(bf16), -1).astype(f32)
    d_kv = d_kv.astype(bf16).astype(f32)
    d_query_lin = rotate(d_query.astype(f32), cosine, -sine_tab).astype(bf16)
    d_second = jnp.where(core == 0, rotate(d_kv, cosine, -sine_tab), d_kv).astype(bf16)

    d_mixed = (dot(d_query_lin, head_q, ROWS) + dot(d_second, head_kv, ROWS)).astype(bf16)
    d_normed = scatter_blocks(d_mixed, TOKEN_AXES, PLANE_SCATTER)
    d_input_part, gain_one = jax.vjp(rms_scale, inputs, gains[0])[1](d_normed)
    grad_tokens = d_middle + d_input_part

    grad_down = uncolumns(grad_down).astype(f32)
    part_out = dot(d_branch_all, heads, FIRST, bf16).reshape(line_count * 8, own, HD)
    grad_out = exchange(after(part_out, grad_down), FINE)
    part_q = dot(normed_all, d_query_lin, FIRST, bf16)
    part_kv = dot(normed_all, d_second, FIRST, bf16)
    part_qkv = jnp.stack(
        [part_q.reshape(line_count * 8, own, HD), part_kv.reshape(line_count * 8, own, HD)], axis=1
    )
    grad_qkv = exchange(after(part_qkv, grad_out), FINE)
    in_back = exchange(after(part_in, grad_qkv), CUBE)
    grad_out = jnp.sum(grad_out.reshape(line_count, 8, own, HD).astype(f32), axis=0)
    grad_out = uncolumns(grad_out)

    qkv_sum = jnp.sum(grad_qkv.reshape(line_count, 16, own, HD).astype(f32), axis=0)
    grad_qkv = qkv_sum.reshape(KVH, 2, 2, own, HD).transpose(0, 2, 1, 3, 4)
    grad_qkv = uncolumns(lax.optimization_barrier(grad_qkv).reshape(16, own, HD))
    grad_in = in_back.transpose(1, 0, 2, 3)
    grad_in = lax.optimization_barrier(grad_in).reshape(16, own, slice_ff)
    grad_in = uncolumns(grad_in).astype(f32)

    grad_gains = sum_all(jnp.stack([gain_one, gain_two, gain_three, gain_four], axis=0))

    tops = tops.astype(f32) + EPSILON
    qkv_tops = tops[0, :, :, : 4 * HD].reshape(KVH, 2, 2, HD).transpose(0, 2, 1, 3).reshape(-1)
    in_tops = tops[..., 4 * HD :].reshape(8, 2, slice_ff).transpose(1, 0, 2).reshape(-1)
    column_scales = jnp.concatenate([qkv_tops, in_tops], axis=0)
    row_scales = jnp.stack([out_scale, down_scale], axis=0)
    return (
        result,
        grad_tokens,
        grad_qkv,
        grad_out,
        grad_in,
        grad_down,
        grad_gains,
        column_scales,
        row_scales,
    )


def solution(mesh):
    fine = Mesh(
        mesh.devices.reshape(mesh.shape["sp"] // 4, 2, 2, mesh.shape["hd"] // 2, 2), FINE
    )
    split = P(FINE, None)
    in_specs = (split, P(), split, split, split, split, P(), split)
    out_specs = (split, split, split, split, split, split, P(), P(), P(None, FINE))
    return jax.shard_map(
        on_device, mesh=fine, in_specs=in_specs, out_specs=out_specs, check_vma=False
    )
```

```python
import math

import jax
import jax.numpy as jnp
import numpy as np
from jax import lax
from jax.experimental import pallas as pl
from jax.experimental.pallas import tpu as pltpu
from jax.sharding import Mesh
from jax.sharding import PartitionSpec as P

FF = 9216
QH = 8
KVH = 4
HD = 256
WINDOW = 4096

EPSILON = 1e-06
SOFTCAP = 50.0
LEVEL_PULL = 0.75
TWO_PI = 2.0 * math.pi

FINE = ("zh", "zl", "x", "y", "c")
LINE = ("zh", "zl")
PLANE = ("x", "y", "c")
CUBE = ("zl", "x", "y")
SWAP = ((0, 1), (1, 0))

SINE = (
    25.13274115538592,
    -64.83582285607088,
    67.07662736368954,
    -38.49587868201696,
    14.049662842567686,
    -3.16160028673954,
)

f32 = jnp.float32
bf16 = jnp.bfloat16


def sin_turns(turns):
    part = turns - jnp.round(turns)
    square = part * part
    poly = SINE[5]
    for factor in SINE[4::-1]:
        poly = poly * square + factor
    return part * (0.25 - square) * poly


def rms_scale(vector_in, gain_row):
    mean_sq = jnp.mean(vector_in * vector_in, axis=-1, keepdims=True)
    return vector_in * lax.rsqrt(mean_sq + EPSILON) * (1.0 + gain_row)


def nested(weight, channel_scale):
    level = weight * (127.0 / channel_scale)
    level = level - (LEVEL_PULL / TWO_PI) * sin_turns(level)
    four = sin_turns(level * (1.0 / 16.0))
    two = sin_turns(level * (1.0 / 64.0))
    total = 3.0 * level - (16.0 * LEVEL_PULL / TWO_PI) * four - (64.0 * LEVEL_PULL / TWO_PI) * two
    return (channel_scale / 381.0) * total


def rotate(vector_in, cosine, sine_tab):
    half_dim = vector_in.shape[-1] // 2
    first_half = vector_in[..., :half_dim]
    second_half = vector_in[..., half_dim:]
    return jnp.concatenate(
        [
            first_half * cosine - second_half * sine_tab,
            second_half * cosine + first_half * sine_tab,
        ],
        axis=-1,
    )


def rope_tables(position, head_dim):
    half_dim = head_dim // 2
    frequency = np.exp(np.arange(half_dim) * (-2.0 * math.log(10000.0) / head_dim)) / TWO_PI
    coarse = frequency.astype(jnp.bfloat16).astype(np.float32)
    fine = (frequency - coarse).astype(np.float32)
    place = position.astype(f32)[:, None]
    turns = place * coarse[None, :]
    turns = (turns - jnp.round(turns)) + place * fine[None, :]
    return (sin_turns(turns + 0.25), sin_turns(turns))


def doc_info(lengths, places):
    stop_at = jnp.cumsum(lengths, dtype=jnp.int32)
    starts = stop_at - lengths
    inside = starts[None, :] <= places[:, None]
    doc_index = jnp.sum(inside.astype(jnp.int32), axis=1) - 1
    doc_start = jnp.max(jnp.where(inside, starts[None, :], 0), axis=1)
    return (doc_index, places - doc_start)


def glu(gate_in, up_in):
    return jax.nn.gelu(gate_in, approximate=True) * up_in


def dot(left, right, dims, out=f32):
    return lax.dot_general(left, right, (dims, ((), ())), preferred_element_type=out)


ROWS = ((1,), (1,))
COLS = ((1,), (0,))
FIRST = ((0,), (0,))


def swap(value, axis):
    return lax.ppermute(value, axis, SWAP)


def gather_blocks(block, axes, orders):
    rows, width = block.shape
    part = width // len(orders)
    parts = []
    for i, order in enumerate(orders):
        held = block[:, i * part : (i + 1) * part].reshape((1,) * len(axes) + (rows, part))
        for axis in order:
            held = jnp.concatenate([held, swap(held, axis)], axis=axes.index(axis))
        parts.append(held)
    return jnp.concatenate(parts, axis=-1).reshape(-1, width)


def scatter_blocks(partial, axes, orders):
    width = partial.shape[-1]
    part = width // len(orders)
    blocks = partial.reshape((2,) * len(axes) + (-1, width))
    parts = []
    for i, order in enumerate(orders):
        held = blocks[..., i * part : (i + 1) * part]
        for axis in order:
            at = axes.index(axis)
            keep = lax.slice_in_dim(held, 0, 1, axis=at)
            send = lax.slice_in_dim(held, 1, 2, axis=at).astype(bf16)
            held = keep.astype(f32) + swap(send, axis).astype(f32)
        parts.append(held.reshape(-1, part))
    return jnp.concatenate(parts, axis=-1)


TOKEN_AXES = ("c", "x", "y")
PLANE_GATHER = (("x", "y", "c"), ("y", "x", "c"))
PLANE_SCATTER = (("c", "y", "x"), ("c", "x", "y"))
CUBE_GATHER = (("zl", "x", "y"), ("x", "y", "zl"), ("y", "zl", "x"))
CUBE_SCATTER = (("y", "x", "zl"), ("zl", "y", "x"), ("x", "zl", "y"))


def after(value, *events):
    return lax.optimization_barrier((value,) + events)[0]


def apart(run, step, *args):
    like = jax.eval_shape(step, *args)

    def nothing(*_):
        return jax.tree.map(lambda leaf: jnp.zeros(leaf.shape, leaf.dtype), like)

    return lax.cond(run, step, nothing, *args)


def both(value, axis):
    other = swap(value, axis)
    first = lax.axis_index(axis) == 0
    return jnp.stack([jnp.where(first, value, other), jnp.where(first, other, value)], axis=0)


def core_sum(grad, own):
    split = grad.reshape(lax.axis_size("zh"), 8, 2, own, grad.shape[-1])
    me = lax.axis_index("c")
    send = lax.dynamic_index_in_dim(split, 1 - me, 2, keepdims=False)
    keep = lax.dynamic_index_in_dim(split, me, 2, keepdims=False)
    return (keep.astype(f32) + swap(send, "c").astype(f32)).astype(bf16)


def line_sum(part):
    flat = part.reshape(-1, part.shape[-1])
    return lax.psum_scatter(flat, "zh", scatter_dimension=0, tiled=True).reshape(part.shape[1:])


def max_both(value, axis):
    return jnp.maximum(value, swap(value, axis))


def sum_all(value):
    for axis in ("c", "x", "y", "zl", "zh"):
        if lax.axis_size(axis) == 2:
            value = value + swap(value, axis)
        else:
            value = lax.psum(value, axis)
    return value


def shift(value, step):
    count = lax.axis_size(LINE)
    return lax.ppermute(value, LINE, [(i, i + step) for i in range(count) if 0 <= i + step < count])


def by_core(part):
    other = swap(part, "c")
    full = jnp.broadcast_to(part[:, :, None], part.shape[:2] + (2,) + part.shape[2:])
    full = lax.dynamic_update_slice_in_dim(full, other[:, :, None], 1 - lax.axis_index("c"), 2)
    return full.reshape(-1, part.shape[-1])


Q_ROWS = 128


def scores(q_ref, k_ref, low_ref, place_ref, k_place_ref):
    raw = dot(q_ref[...], k_ref[...], ROWS) * (1.0 / (math.sqrt(HD) * SOFTCAP))
    places = k_place_ref[...]
    allowed = (places >= low_ref[...]) & (places <= place_ref[...])
    return jnp.tanh(raw), allowed


def attend_kernel(q_ref, k_ref, v_ref, low_ref, place_ref, k_place_ref, out_ref, lse_ref):
    tanh_part, allowed = scores(q_ref, k_ref, low_ref, place_ref, k_place_ref)
    capped = jnp.where(allowed, SOFTCAP * tanh_part, -1e30)
    row_max = jnp.max(capped, axis=1, keepdims=True)
    exp_scores = jnp.exp(capped - row_max)
    row_total = jnp.sum(exp_scores, axis=1, keepdims=True)
    probs = (exp_scores * (1.0 / row_total)).astype(bf16)
    out_ref[...] = dot(probs, v_ref[...], COLS).astype(bf16)
    lse_ref[...] = row_max + jnp.log(row_total)


def attend_back_kernel(
    q_ref, k_ref, v_ref, low_ref, place_ref, k_place_ref, lse_ref, d_ref, dq_ref, dk_ref, dv_ref
):
    @pl.when(pl.program_id(0) == 0)
    def _():
        dk_ref[...] = jnp.zeros_like(dk_ref)
        dv_ref[...] = jnp.zeros_like(dv_ref)

    scale = 1.0 / math.sqrt(HD)
    tanh_part, allowed = scores(q_ref, k_ref, low_ref, place_ref, k_place_ref)
    probs = jnp.where(allowed, jnp.exp(SOFTCAP * tanh_part - lse_ref[...]), 0.0)
    dv_ref[...] += dot(probs.astype(bf16), d_ref[...], FIRST)
    d_prob = dot(d_ref[...], v_ref[...], ROWS)
    delta = jnp.sum(probs * d_prob, axis=1, keepdims=True)
    d_raw = (probs * (d_prob - delta) * (1.0 - tanh_part * tanh_part)).astype(bf16)
    dq_ref[...] = (dot(d_raw, k_ref[...], COLS) * scale).astype(bf16)
    dk_ref[...] += dot(d_raw, q_ref[...], FIRST) * scale


def attention_specs(rows, keys):
    q_spec = pl.BlockSpec((Q_ROWS, HD), lambda i: (i, 0))
    k_spec = pl.BlockSpec((keys, HD), lambda i: (0, 0))
    row_spec = pl.BlockSpec((Q_ROWS, 1), lambda i: (i, 0))
    place_spec = pl.BlockSpec((1, keys), lambda i: (0, 0))
    common = dict(
        grid=(rows // Q_ROWS,),
        compiler_params=pltpu.CompilerParams(
            dimension_semantics=("arbitrary",), vmem_limit_bytes=56 * 2**20
        ),
        cost_estimate=pl.CostEstimate(flops=1, bytes_accessed=1, transcendentals=0),
    )
    return q_spec, k_spec, row_spec, place_spec, common


def attend(query, key_rows, value_rows, low, place, k_place):
    rows, keys = query.shape[0], key_rows.shape[0]
    q_spec, k_spec, row_spec, place_spec, common = attention_specs(rows, keys)
    return pl.pallas_call(
        attend_kernel,
        out_shape=(
            jax.ShapeDtypeStruct((rows, HD), bf16),
            jax.ShapeDtypeStruct((rows, 1), f32),
        ),
        in_specs=[q_spec, k_spec, k_spec, row_spec, row_spec, place_spec],
        out_specs=(q_spec, row_spec),
        **common,
    )(query, key_rows, value_rows, low, place, k_place)


def attend_back(query, key_rows, value_rows, low, place, k_place, lse, d_heads):
    rows, keys = query.shape[0], key_rows.shape[0]
    q_spec, k_spec, row_spec, place_spec, common = attention_specs(rows, keys)
    return pl.pallas_call(
        attend_back_kernel,
        out_shape=(
            jax.ShapeDtypeStruct((rows, HD), bf16),
            jax.ShapeDtypeStruct((keys, HD), f32),
            jax.ShapeDtypeStruct((keys, HD), f32),
        ),
        in_specs=[q_spec, k_spec, k_spec, row_spec, row_spec, place_spec, row_spec, q_spec],
        out_specs=(q_spec, k_spec, k_spec),
        **common,
    )(query, key_rows, value_rows, low, place, k_place, lse, d_heads)


def exchange(value, axes):
    return lax.all_to_all(value, axes, split_axis=0, concat_axis=0, tiled=True)


def columns(weight, count):
    own, width = weight.shape
    return weight.reshape(own, count, width // count).transpose(1, 0, 2)


def uncolumns(parts):
    count, own, width = parts.shape
    return parts.transpose(1, 0, 2).reshape(own, count * width)


def on_device(tokens, gains, w_qkv, w_out, w_in, w_down, lengths, cotangent):
    line_count = lax.axis_size(LINE)
    line_index = lax.axis_index(LINE)
    core = lax.axis_index("c")
    x_index = lax.axis_index("x")
    y_index = lax.axis_index("y")
    tok_rows, model = tokens.shape
    own = w_qkv.shape[0]
    block_rows = 8 * tok_rows
    total_rows = line_count * block_rows
    slice_ff = FF // 8
    run = lengths[0] > 0

    units = lax.optimization_barrier(columns(w_qkv, 16)).reshape(KVH, 2, 2, own, HD)
    qkv_out = units.transpose(0, 2, 1, 3, 4).reshape(8, 2, own, HD)
    qkv_out = jnp.broadcast_to(qkv_out[None], (line_count, 8, 2, own, HD))
    qkv_lat = exchange(qkv_out.reshape(line_count * 8, 2, own, HD), FINE)
    qkv_lat = qkv_lat.reshape(line_count, 8, 2, own, HD)

    inputs = tokens.astype(f32)
    normed = rms_scale(inputs, gains[0]).astype(bf16)
    def gather_plane(block):
        return gather_blocks(block, TOKEN_AXES, PLANE_GATHER)

    def scatter_plane(partial):
        return scatter_blocks(partial, TOKEN_AXES, PLANE_SCATTER)

    def gather_cube(block):
        return gather_blocks(block, CUBE, CUBE_GATHER)

    def scatter_cube(partial):
        return scatter_blocks(partial, CUBE, CUBE_SCATTER)

    normed_all = apart(run, gather_plane, normed)

    out_scale = jnp.max(jnp.abs(w_out.astype(f32)), axis=1) + EPSILON
    down_scale = jnp.max(jnp.abs(w_down.astype(f32)), axis=1) + EPSILON
    eff_out = nested(w_out.astype(f32), out_scale[:, None]).astype(bf16)
    eff_down = nested(w_down.astype(f32), down_scale[:, None]).astype(bf16)
    eff_out = jnp.broadcast_to(columns(eff_out, 8)[None], (line_count, 8, own, HD))
    head_out = after(eff_out.reshape(line_count * 8, own, HD), qkv_lat, normed_all)
    head_out = exchange(head_out, FINE)

    def spread(weight, *events):
        cols = jnp.broadcast_to(weight[None], (lax.axis_size("zh"),) + weight.shape)
        cols = after(cols.reshape(-1, own, slice_ff), *events)
        return exchange(cols, LINE + ("x", "y")).reshape(-1, 8, own, slice_ff)

    head_out = head_out.reshape(model, HD)

    qkv_max = jnp.max(jnp.abs(qkv_lat), axis=(0, 1, 3))
    qkv_scale = qkv_max.astype(f32) + EPSILON
    head_qkv = nested(qkv_lat.astype(f32), qkv_scale[None, None, :, None, :]).astype(bf16)
    head_q = head_qkv[:, :, 0].reshape(model, HD)
    head_kv = head_qkv[:, :, 1].reshape(model, HD)

    dev = jnp.arange(8, dtype=jnp.int32)
    dev = (
        ((dev // 2 % 2) ^ x_index) * 4 + ((dev % 2) ^ y_index) * 2 + ((dev // 4) ^ core)
    ).astype(jnp.int32)
    inner = (dev[:, None] * tok_rows + jnp.arange(tok_rows, dtype=jnp.int32)[None, :]).reshape(-1)
    q_places = line_index * block_rows + inner
    position = doc_info(lengths, q_places)[1]
    cosine, sine_tab = rope_tables(position, HD)

    second = dot(normed_all, head_kv, COLS)
    kv_own = jnp.where(core == 0, rotate(second, cosine, sine_tab), second).astype(bf16)

    reach = min(WINDOW, total_rows // 2)
    back = min(line_count - 1, -(-(reach - 1) // block_rows))
    half_block = block_rows // 2

    def flip(value):
        return jnp.concatenate([value[:, half_block:], value[:, :half_block]], axis=1)

    def pass_up(own_rows):
        shifted = [own_rows]
        for _ in range(back):
            shifted.append(shift(shifted[-1], 1))
        mine = jnp.stack(shifted[::-1], axis=0)
        other = flip(swap(mine, "c"))
        keys = jnp.where(core == 0, mine, other).reshape(-1, HD)
        values = jnp.where(core == 0, other, mine).reshape(-1, HD)
        return keys, values

    key_rows, value_rows = apart(run, pass_up, kv_own)
    query = rotate(dot(normed_all, head_q, COLS), cosine, sine_tab).astype(bf16)

    gate_lat = spread(columns(w_in[:, :FF], 8), head_out, key_rows)
    def effective(lat):
        top = max_both(jnp.max(jnp.abs(lat), axis=(0, 1, 2)), "c")
        return top, by_core(nested(lat.astype(f32), top.astype(f32) + EPSILON).astype(bf16))

    k_places = jnp.concatenate(
        [q_places - n * block_rows for n in range(back, -1, -1)], axis=0
    )
    place = q_places[:, None]
    low = jnp.maximum(q_places - position, q_places - (WINDOW - 1))[:, None]
    heads, lse = attend(query, key_rows, value_rows, low, place, k_places[None])

    branch = dot(heads, head_out, ROWS, bf16)

    branch = apart(run, scatter_plane, branch)
    up_lat = spread(columns(w_in[:, FF:], 8), gate_lat, branch)
    middle = inputs + rms_scale(branch, gains[1])
    pre_mlp = rms_scale(middle, gains[2]).astype(bf16)
    pre_all = apart(run, gather_cube, pre_mlp)
    gate_top, cols_gate = apart(run, effective, after(gate_lat, pre_all))
    down_lat = spread(columns(eff_down, 8), up_lat, cols_gate)
    up_top, cols_up = apart(run, effective, after(up_lat, cols_gate))
    pre_turned = lax.optimization_barrier(pre_all.T)
    gate_part = dot(pre_all, cols_gate, COLS)
    up_part = dot(pre_all, cols_up, COLS)
    hidden = glu(gate_part, up_part).astype(bf16)
    cols_down = apart(run, by_core, after(down_lat, gate_part, up_part))
    down_out = apart(run, scatter_cube, dot(hidden, cols_down, ROWS, bf16))
    result = (middle + rms_scale(down_out, gains[3])).astype(bf16)

    grad_result = cotangent.astype(f32)
    d_down, gain_four = jax.vjp(rms_scale, down_out, gains[3])[1](grad_result)
    d_down = d_down.astype(bf16)

    def gather_down(block, qkv_row, in_row):
        tops = jnp.concatenate([both(qkv_row, "c").reshape(-1), in_row], axis=0)
        return gather_cube(block), both(both(both(tops, "y"), "x"), "zl")

    d_down_all, tops = apart(
        run, gather_down, d_down, qkv_max.reshape(-1), jnp.concatenate([gate_top, up_top])
    )

    def hidden_back(d_down_all, hidden, gate_part, up_part, cols_down):
        part = dot(d_down_all, hidden, FIRST, bf16)
        d_hidden = dot(after(d_down_all, part), cols_down, COLS)
        d_gate, d_up = jax.vjp(glu, gate_part, up_part)[1](d_hidden)
        return core_sum(part, own), d_gate.astype(bf16), d_up.astype(bf16)

    part_down, d_gate, d_up = apart(
        run, hidden_back, d_down_all, hidden, gate_part, up_part, cols_down
    )

    def collect(part, *events):
        flat = after(part.reshape(-1, own, slice_ff), *events)
        return exchange(flat, LINE + ("x", "y")).reshape(-1, 8, own, slice_ff)

    down_back = collect(part_down)
    d_pre = (dot(d_gate, cols_gate, ROWS) + dot(d_up, cols_up, ROWS)).astype(bf16)

    def scatter_pre(partial, gate, up):
        return scatter_cube(partial), core_sum(gate, own), core_sum(up, own)

    d_pre, part_gate, part_up = apart(
        run, scatter_pre, d_pre, dot(pre_turned, d_gate, COLS, bf16), dot(pre_turned, d_up, COLS, bf16)
    )
    gate_back = collect(part_gate, down_back)
    d_mid_part, gain_three = jax.vjp(rms_scale, middle, gains[2])[1](d_pre)
    d_middle = grad_result + d_mid_part
    d_branch, gain_two = jax.vjp(rms_scale, branch, gains[1])[1](d_middle)
    d_branch_all = apart(run, gather_plane, d_branch.astype(bf16))
    up_back = collect(part_up, gate_back, d_branch_all)
    d_heads = dot(d_branch_all, head_out, COLS).astype(bf16)

    d_query, d_keys, d_values = attend_back(
        query, key_rows, value_rows, low, place, k_places[None], lse, d_heads
    )

    def pass_down(d_keys, d_values):
        d_keys = d_keys.reshape(back + 1, block_rows, HD)
        d_values = d_values.reshape(back + 1, block_rows, HD)
        send = flip(jnp.where(core == 0, d_values, d_keys).astype(bf16))
        window = jnp.where(core == 0, d_keys, d_values) + swap(send, "c").astype(f32)
        total = window[0]
        for n in range(1, back + 1):
            total = window[n] + shift(total.astype(bf16), -1).astype(f32)
        return total.astype(bf16)

    d_kv = apart(run, pass_down, d_keys, d_values).astype(f32)
    d_query_lin = rotate(d_query.astype(f32), cosine, -sine_tab).astype(bf16)
    d_second = jnp.where(core == 0, rotate(d_kv, cosine, -sine_tab), d_kv).astype(bf16)

    d_mixed = (dot(d_query_lin, head_q, ROWS) + dot(d_second, head_kv, ROWS)).astype(bf16)
    d_normed = apart(run, scatter_plane, d_mixed)
    d_input_part, gain_one = jax.vjp(rms_scale, inputs, gains[0])[1](d_normed)
    grad_tokens = d_middle + d_input_part

    parts = [dot(normed_all, d_query_lin, FIRST, bf16), dot(normed_all, d_second, FIRST, bf16)]
    parts.append(dot(d_branch_all, heads, FIRST, bf16))
    parts = jnp.stack([part.reshape(line_count * 8, own, HD) for part in parts], axis=1)
    sums = exchange(after(parts, up_back), FINE).reshape(line_count, 8, 3, own, HD)
    sums = jnp.sum(sums.astype(f32), axis=0)
    grad_out = uncolumns(sums[:, 2])
    grad_qkv = sums[:, :2].reshape(KVH, 2, 2, own, HD).transpose(0, 2, 1, 3, 4)
    grad_qkv = uncolumns(lax.optimization_barrier(grad_qkv).reshape(16, own, HD))

    def owned(back):
        return uncolumns(jnp.sum(back.astype(f32), axis=0))

    grad_in = jnp.concatenate([owned(gate_back), owned(up_back)], axis=1)
    grad_down = owned(down_back)

    grad_gains = apart(run, sum_all, jnp.stack([gain_one, gain_two, gain_three, gain_four], axis=0))

    tops = tops.astype(f32) + EPSILON
    qkv_tops = tops[0, :, :, : 4 * HD].reshape(KVH, 2, 2, HD).transpose(0, 2, 1, 3).reshape(-1)
    in_tops = tops[..., 4 * HD :].reshape(8, 2, slice_ff).transpose(1, 0, 2).reshape(-1)
    column_scales = jnp.concatenate([qkv_tops, in_tops], axis=0)
    row_scales = jnp.stack([out_scale, down_scale], axis=0)
    return (
        result,
        grad_tokens,
        grad_qkv,
        grad_out,
        grad_in,
        grad_down,
        grad_gains,
        column_scales,
        row_scales,
    )


def solution(mesh):
    fine = Mesh(
        mesh.devices.reshape(mesh.shape["sp"] // 4, 2, 2, mesh.shape["hd"] // 2, 2), FINE
    )
    split = P(FINE, None)
    in_specs = (split, P(), split, split, split, split, P(), split)
    out_specs = (split, split, split, split, split, split, P(), P(), P(None, FINE))
    return jax.shard_map(
        on_device, mesh=fine, in_specs=in_specs, out_specs=out_specs, check_vma=False
    )
```

```python
import math

import jax
import jax.numpy as jnp
import numpy as np
from jax import lax
from jax.experimental import pallas as pl
from jax.experimental.pallas import tpu as pltpu
from jax.sharding import Mesh
from jax.sharding import PartitionSpec as P

FF = 9216
QH = 8
KVH = 4
HD = 256
WINDOW = 4096

EPSILON = 1e-06
SOFTCAP = 50.0
LEVEL_PULL = 0.75
TWO_PI = 2.0 * math.pi

FINE = ("zh", "zl", "x", "y", "c")
LINE = ("zh", "zl")
PLANE = ("x", "y", "c")
CUBE = ("zl", "x", "y")
SWAP = ((0, 1), (1, 0))

SINE = (
    25.13274115538592,
    -64.83582285607088,
    67.07662736368954,
    -38.49587868201696,
    14.049662842567686,
    -3.16160028673954,
)

f32 = jnp.float32
bf16 = jnp.bfloat16


def sin_turns(turns):
    part = turns - jnp.round(turns)
    square = part * part
    poly = SINE[5]
    for factor in SINE[4::-1]:
        poly = poly * square + factor
    return part * (0.25 - square) * poly


def rms_scale(vector_in, gain_row):
    mean_sq = jnp.mean(vector_in * vector_in, axis=-1, keepdims=True)
    return vector_in * lax.rsqrt(mean_sq + EPSILON) * (1.0 + gain_row)


def nested(weight, channel_scale):
    level = weight * (127.0 / channel_scale)
    level = level - (LEVEL_PULL / TWO_PI) * sin_turns(level)
    four = sin_turns(level * (1.0 / 16.0))
    two = sin_turns(level * (1.0 / 64.0))
    total = 3.0 * level - (16.0 * LEVEL_PULL / TWO_PI) * four - (64.0 * LEVEL_PULL / TWO_PI) * two
    return (channel_scale / 381.0) * total


def rotate(vector_in, cosine, sine_tab):
    half_dim = vector_in.shape[-1] // 2
    first_half = vector_in[..., :half_dim]
    second_half = vector_in[..., half_dim:]
    return jnp.concatenate(
        [
            first_half * cosine - second_half * sine_tab,
            second_half * cosine + first_half * sine_tab,
        ],
        axis=-1,
    )


def rope_tables(position, head_dim):
    half_dim = head_dim // 2
    frequency = np.exp(np.arange(half_dim) * (-2.0 * math.log(10000.0) / head_dim)) / TWO_PI
    coarse = frequency.astype(jnp.bfloat16).astype(np.float32)
    fine = (frequency - coarse).astype(np.float32)
    place = position.astype(f32)[:, None]
    turns = place * coarse[None, :]
    turns = (turns - jnp.round(turns)) + place * fine[None, :]
    return (sin_turns(turns + 0.25), sin_turns(turns))


def doc_info(lengths, places):
    stop_at = jnp.cumsum(lengths, dtype=jnp.int32)
    starts = stop_at - lengths
    inside = starts[None, :] <= places[:, None]
    doc_index = jnp.sum(inside.astype(jnp.int32), axis=1) - 1
    doc_start = jnp.max(jnp.where(inside, starts[None, :], 0), axis=1)
    return (doc_index, places - doc_start)


def glu(gate_in, up_in):
    return jax.nn.gelu(gate_in, approximate=True) * up_in


def dot(left, right, dims, out=f32):
    return lax.dot_general(left, right, (dims, ((), ())), preferred_element_type=out)


ROWS = ((1,), (1,))
COLS = ((1,), (0,))
FIRST = ((0,), (0,))


def swap(value, axis):
    return lax.ppermute(value, axis, SWAP)


def gather_blocks(block, axes, orders):
    rows, width = block.shape
    part = width // len(orders)
    parts = []
    for i, order in enumerate(orders):
        held = block[:, i * part : (i + 1) * part].reshape((1,) * len(axes) + (rows, part))
        for axis in order:
            held = jnp.concatenate([held, swap(held, axis)], axis=axes.index(axis))
        parts.append(held)
    return jnp.concatenate(parts, axis=-1).reshape(-1, width)


def scatter_blocks(partial, axes, orders):
    width = partial.shape[-1]
    part = width // len(orders)
    blocks = partial.reshape((2,) * len(axes) + (-1, width))
    parts = []
    for i, order in enumerate(orders):
        held = blocks[..., i * part : (i + 1) * part]
        for axis in order:
            at = axes.index(axis)
            keep = lax.slice_in_dim(held, 0, 1, axis=at)
            send = lax.slice_in_dim(held, 1, 2, axis=at).astype(bf16)
            held = keep.astype(f32) + swap(send, axis).astype(f32)
        parts.append(held.reshape(-1, part))
    return jnp.concatenate(parts, axis=-1)


TOKEN_AXES = ("c", "x", "y")
PLANE_GATHER = (("x", "y", "c"), ("y", "x", "c"))
PLANE_SCATTER = (("c", "y", "x"), ("c", "x", "y"))
CUBE_GATHER = (("zl", "x", "y"), ("x", "y", "zl"), ("y", "zl", "x"))
CUBE_SCATTER = (("y", "x", "zl"), ("zl", "y", "x"), ("x", "zl", "y"))


def after(value, *events):
    return lax.optimization_barrier((value,) + events)[0]


def apart(run, step, *args):
    like = jax.eval_shape(step, *args)

    def nothing(*_):
        return jax.tree.map(lambda leaf: jnp.zeros(leaf.shape, leaf.dtype), like)

    return lax.cond(run, step, nothing, *args)


def both(value, axis):
    other = swap(value, axis)
    first = lax.axis_index(axis) == 0
    return jnp.stack([jnp.where(first, value, other), jnp.where(first, other, value)], axis=0)


def core_sum(grad, own):
    split = grad.reshape(lax.axis_size("zh"), 8, 2, own, grad.shape[-1])
    me = lax.axis_index("c")
    send = lax.dynamic_index_in_dim(split, 1 - me, 2, keepdims=False)
    keep = lax.dynamic_index_in_dim(split, me, 2, keepdims=False)
    return (keep.astype(f32) + swap(send, "c").astype(f32)).astype(bf16)


def line_sum(part):
    flat = part.reshape(-1, part.shape[-1])
    return lax.psum_scatter(flat, "zh", scatter_dimension=0, tiled=True).reshape(part.shape[1:])


def max_both(value, axis):
    return jnp.maximum(value, swap(value, axis))


def sum_all(value):
    for axis in ("c", "x", "y", "zl", "zh"):
        if lax.axis_size(axis) == 2:
            value = value + swap(value, axis)
        else:
            value = lax.psum(value, axis)
    return value


def shift(value, step):
    count = lax.axis_size(LINE)
    return lax.ppermute(value, LINE, [(i, i + step) for i in range(count) if 0 <= i + step < count])


def by_core(part):
    other = swap(part, "c")
    full = jnp.broadcast_to(part[:, :, None], part.shape[:2] + (2,) + part.shape[2:])
    full = lax.dynamic_update_slice_in_dim(full, other[:, :, None], 1 - lax.axis_index("c"), 2)
    return full.reshape(-1, part.shape[-1])


Q_ROWS = 128


def scores(q_ref, k_ref, low_ref, place_ref, k_place_ref):
    raw = dot(q_ref[...], k_ref[...], ROWS) * (1.0 / (math.sqrt(HD) * SOFTCAP))
    places = k_place_ref[...]
    allowed = (places >= low_ref[...]) & (places <= place_ref[...])
    return jnp.tanh(raw), allowed


def attend_kernel(q_ref, k_ref, v_ref, low_ref, place_ref, k_place_ref, out_ref, lse_ref):
    tanh_part, allowed = scores(q_ref, k_ref, low_ref, place_ref, k_place_ref)
    capped = jnp.where(allowed, SOFTCAP * tanh_part, -1e30)
    row_max = jnp.max(capped, axis=1, keepdims=True)
    exp_scores = jnp.exp(capped - row_max)
    row_total = jnp.sum(exp_scores, axis=1, keepdims=True)
    probs = (exp_scores * (1.0 / row_total)).astype(bf16)
    out_ref[...] = dot(probs, v_ref[...], COLS).astype(bf16)
    lse_ref[...] = row_max + jnp.log(row_total)


def attend_back_kernel(
    q_ref, k_ref, v_ref, low_ref, place_ref, k_place_ref, lse_ref, d_ref, dq_ref, dk_ref, dv_ref
):
    @pl.when(pl.program_id(0) == 0)
    def _():
        dk_ref[...] = jnp.zeros_like(dk_ref)
        dv_ref[...] = jnp.zeros_like(dv_ref)

    scale = 1.0 / math.sqrt(HD)
    tanh_part, allowed = scores(q_ref, k_ref, low_ref, place_ref, k_place_ref)
    probs = jnp.where(allowed, jnp.exp(SOFTCAP * tanh_part - lse_ref[...]), 0.0)
    dv_ref[...] += dot(probs.astype(bf16), d_ref[...], FIRST)
    d_prob = dot(d_ref[...], v_ref[...], ROWS)
    delta = jnp.sum(probs * d_prob, axis=1, keepdims=True)
    d_raw = (probs * (d_prob - delta) * (1.0 - tanh_part * tanh_part)).astype(bf16)
    dq_ref[...] = (dot(d_raw, k_ref[...], COLS) * scale).astype(bf16)
    dk_ref[...] += dot(d_raw, q_ref[...], FIRST) * scale


def attention_specs(rows, keys):
    q_spec = pl.BlockSpec((Q_ROWS, HD), lambda i: (i, 0))
    k_spec = pl.BlockSpec((keys, HD), lambda i: (0, 0))
    row_spec = pl.BlockSpec((Q_ROWS, 1), lambda i: (i, 0))
    place_spec = pl.BlockSpec((1, keys), lambda i: (0, 0))
    common = dict(
        grid=(rows // Q_ROWS,),
        compiler_params=pltpu.CompilerParams(
            dimension_semantics=("arbitrary",), vmem_limit_bytes=56 * 2**20
        ),
        cost_estimate=pl.CostEstimate(flops=1, bytes_accessed=1, transcendentals=0),
    )
    return q_spec, k_spec, row_spec, place_spec, common


def attend(query, key_rows, value_rows, low, place, k_place):
    rows, keys = query.shape[0], key_rows.shape[0]
    q_spec, k_spec, row_spec, place_spec, common = attention_specs(rows, keys)
    return pl.pallas_call(
        attend_kernel,
        out_shape=(
            jax.ShapeDtypeStruct((rows, HD), bf16),
            jax.ShapeDtypeStruct((rows, 1), f32),
        ),
        in_specs=[q_spec, k_spec, k_spec, row_spec, row_spec, place_spec],
        out_specs=(q_spec, row_spec),
        **common,
    )(query, key_rows, value_rows, low, place, k_place)


def attend_back(query, key_rows, value_rows, low, place, k_place, lse, d_heads):
    rows, keys = query.shape[0], key_rows.shape[0]
    q_spec, k_spec, row_spec, place_spec, common = attention_specs(rows, keys)
    return pl.pallas_call(
        attend_back_kernel,
        out_shape=(
            jax.ShapeDtypeStruct((rows, HD), bf16),
            jax.ShapeDtypeStruct((keys, HD), f32),
            jax.ShapeDtypeStruct((keys, HD), f32),
        ),
        in_specs=[q_spec, k_spec, k_spec, row_spec, row_spec, place_spec, row_spec, q_spec],
        out_specs=(q_spec, k_spec, k_spec),
        **common,
    )(query, key_rows, value_rows, low, place, k_place, lse, d_heads)


def exchange(value, axes):
    return lax.all_to_all(value, axes, split_axis=0, concat_axis=0, tiled=True)


def columns(weight, count):
    own, width = weight.shape
    return weight.reshape(own, count, width // count).transpose(1, 0, 2)


def uncolumns(parts):
    count, own, width = parts.shape
    return parts.transpose(1, 0, 2).reshape(own, count * width)


def on_device(tokens, gains, w_qkv, w_out, w_in, w_down, lengths, cotangent):
    line_count = lax.axis_size(LINE)
    line_index = lax.axis_index(LINE)
    core = lax.axis_index("c")
    x_index = lax.axis_index("x")
    y_index = lax.axis_index("y")
    tok_rows, model = tokens.shape
    own = w_qkv.shape[0]
    block_rows = 8 * tok_rows
    total_rows = line_count * block_rows
    slice_ff = FF // 8
    run = lengths[0] > 0

    units = lax.optimization_barrier(columns(w_qkv, 16)).reshape(KVH, 2, 2, own, HD)
    qkv_out = units.transpose(0, 2, 1, 3, 4).reshape(8, 2, own, HD)
    qkv_out = jnp.broadcast_to(qkv_out[None], (line_count, 8, 2, own, HD))
    qkv_lat = exchange(qkv_out.reshape(line_count * 8, 2, own, HD), FINE)
    qkv_lat = qkv_lat.reshape(line_count, 8, 2, own, HD)

    inputs = tokens.astype(f32)
    normed = rms_scale(inputs, gains[0]).astype(bf16)
    def gather_plane(block):
        return gather_blocks(block, TOKEN_AXES, PLANE_GATHER)

    def scatter_plane(partial):
        return scatter_blocks(partial, TOKEN_AXES, PLANE_SCATTER)

    def gather_cube(block):
        return gather_blocks(block, CUBE, CUBE_GATHER)

    def scatter_cube(partial):
        return scatter_blocks(partial, CUBE, CUBE_SCATTER)

    normed_all = apart(run, gather_plane, normed)

    out_scale = jnp.max(jnp.abs(w_out.astype(f32)), axis=1) + EPSILON
    down_scale = jnp.max(jnp.abs(w_down.astype(f32)), axis=1) + EPSILON
    eff_out = nested(w_out.astype(f32), out_scale[:, None]).astype(bf16)
    eff_down = nested(w_down.astype(f32), down_scale[:, None]).astype(bf16)
    eff_out = jnp.broadcast_to(columns(eff_out, 8)[None], (line_count, 8, own, HD))
    head_out = after(eff_out.reshape(line_count * 8, own, HD), qkv_lat, normed_all)
    head_out = exchange(head_out, FINE)

    def spread(weight, *events):
        cols = jnp.broadcast_to(weight[None], (lax.axis_size("zh"),) + weight.shape)
        cols = after(cols.reshape(-1, own, slice_ff), *events)
        return exchange(cols, LINE + ("x", "y")).reshape(-1, 8, own, slice_ff)

    head_out = head_out.reshape(model, HD)

    qkv_max = jnp.max(jnp.abs(qkv_lat), axis=(0, 1, 3))
    qkv_scale = qkv_max.astype(f32) + EPSILON
    head_qkv = nested(qkv_lat.astype(f32), qkv_scale[None, None, :, None, :]).astype(bf16)
    head_q = head_qkv[:, :, 0].reshape(model, HD)
    head_kv = head_qkv[:, :, 1].reshape(model, HD)

    dev = jnp.arange(8, dtype=jnp.int32)
    dev = (
        ((dev // 2 % 2) ^ x_index) * 4 + ((dev % 2) ^ y_index) * 2 + ((dev // 4) ^ core)
    ).astype(jnp.int32)
    inner = (dev[:, None] * tok_rows + jnp.arange(tok_rows, dtype=jnp.int32)[None, :]).reshape(-1)
    q_places = line_index * block_rows + inner
    position = doc_info(lengths, q_places)[1]
    cosine, sine_tab = rope_tables(position, HD)

    second = dot(normed_all, head_kv, COLS)
    kv_own = jnp.where(core == 0, rotate(second, cosine, sine_tab), second).astype(bf16)

    reach = min(WINDOW, total_rows // 2)
    back = min(line_count - 1, -(-(reach - 1) // block_rows))
    half_block = block_rows // 2

    def flip(value):
        return jnp.concatenate([value[:, half_block:], value[:, :half_block]], axis=1)

    def pass_up(own_rows, normed_all, head_q, cosine, sine_tab):
        query = rotate(dot(normed_all, head_q, COLS), cosine, sine_tab).astype(bf16)
        shifted = [own_rows]
        for _ in range(back):
            shifted.append(shift(shifted[-1], 1))
        mine = jnp.stack(shifted[::-1], axis=0)
        other = flip(swap(mine, "c"))
        keys = jnp.where(core == 0, mine, other).reshape(-1, HD)
        values = jnp.where(core == 0, other, mine).reshape(-1, HD)
        return keys, values, query

    key_rows, value_rows, query = apart(
        run, pass_up, kv_own, normed_all, head_q, cosine, sine_tab
    )

    gate_lat = spread(columns(w_in[:, :FF], 8), head_out, key_rows)
    def effective(lat):
        top = max_both(jnp.max(jnp.abs(lat), axis=(0, 1, 2)), "c")
        return top, by_core(nested(lat.astype(f32), top.astype(f32) + EPSILON).astype(bf16))

    k_places = jnp.concatenate(
        [q_places - n * block_rows for n in range(back, -1, -1)], axis=0
    )
    place = q_places[:, None]
    low = jnp.maximum(q_places - position, q_places - (WINDOW - 1))[:, None]
    heads, lse = attend(query, key_rows, value_rows, low, place, k_places[None])

    branch = dot(heads, head_out, ROWS, bf16)

    branch = apart(run, scatter_plane, branch)
    up_lat = spread(columns(w_in[:, FF:], 8), gate_lat, branch)
    middle = inputs + rms_scale(branch, gains[1])
    pre_mlp = rms_scale(middle, gains[2]).astype(bf16)
    pre_all = apart(run, gather_cube, pre_mlp)
    down_lat = spread(columns(eff_down, 8), up_lat, pre_all)

    def both_effective(gate_lat, up_lat):
        gate_top, cols_gate = effective(gate_lat)
        up_top, cols_up = effective(up_lat)
        return cols_gate, cols_up, jnp.concatenate([gate_top, up_top])

    cols_gate, cols_up, in_tops = apart(run, both_effective, after(gate_lat, pre_all), up_lat)
    pre_turned = lax.optimization_barrier(pre_all.T)
    gate_part = dot(pre_all, cols_gate, COLS)
    up_part = dot(pre_all, cols_up, COLS)
    cols_down = apart(run, by_core, after(down_lat, gate_part, up_part))
    hidden = glu(gate_part, up_part).astype(bf16)
    down_out = apart(run, scatter_cube, dot(hidden, cols_down, ROWS, bf16))
    result = (middle + rms_scale(down_out, gains[3])).astype(bf16)

    grad_result = cotangent.astype(f32)
    d_down, gain_four = jax.vjp(rms_scale, down_out, gains[3])[1](grad_result)
    d_down = d_down.astype(bf16)

    def gather_down(block, qkv_row, in_row):
        tops = jnp.concatenate([both(qkv_row, "c").reshape(-1), in_row], axis=0)
        return gather_cube(block), both(both(both(tops, "y"), "x"), "zl")

    d_down_all, tops = apart(
        run, gather_down, d_down, qkv_max.reshape(-1), in_tops
    )

    def hidden_back(d_down_all, hidden, gate_part, up_part, cols_down):
        part = dot(d_down_all, hidden, FIRST, bf16)
        d_hidden = dot(after(d_down_all, part), cols_down, COLS)
        d_gate, d_up = jax.vjp(glu, gate_part, up_part)[1](d_hidden)
        return core_sum(part, own), d_gate.astype(bf16), d_up.astype(bf16)

    part_down, d_gate, d_up = apart(
        run, hidden_back, d_down_all, hidden, gate_part, up_part, cols_down
    )

    def collect(part, *events):
        flat = after(part.reshape(-1, own, slice_ff), *events)
        return exchange(flat, LINE + ("x", "y")).reshape(-1, 8, own, slice_ff)

    down_back = collect(part_down)
    d_pre = (dot(d_gate, cols_gate, ROWS) + dot(d_up, cols_up, ROWS)).astype(bf16)

    def scatter_pre(partial, gate, up):
        return scatter_cube(partial), core_sum(gate, own), core_sum(up, own)

    d_pre, part_gate, part_up = apart(
        run, scatter_pre, d_pre, dot(pre_turned, d_gate, COLS, bf16), dot(pre_turned, d_up, COLS, bf16)
    )
    gate_back = collect(part_gate, down_back)
    d_mid_part, gain_three = jax.vjp(rms_scale, middle, gains[2])[1](d_pre)
    d_middle = grad_result + d_mid_part
    d_branch, gain_two = jax.vjp(rms_scale, branch, gains[1])[1](d_middle)
    d_branch_all = apart(run, gather_plane, d_branch.astype(bf16))
    up_back = collect(part_up, gate_back, d_branch_all)
    d_heads = dot(d_branch_all, head_out, COLS).astype(bf16)

    d_query, d_keys, d_values = attend_back(
        query, key_rows, value_rows, low, place, k_places[None], lse, d_heads
    )

    def pass_down(d_keys, d_values):
        d_keys = d_keys.reshape(back + 1, block_rows, HD)
        d_values = d_values.reshape(back + 1, block_rows, HD)
        send = flip(jnp.where(core == 0, d_values, d_keys).astype(bf16))
        window = jnp.where(core == 0, d_keys, d_values) + swap(send, "c").astype(f32)
        total = window[0]
        for n in range(1, back + 1):
            total = window[n] + shift(total.astype(bf16), -1).astype(f32)
        return total.astype(bf16)

    d_kv = apart(run, pass_down, d_keys, d_values).astype(f32)
    d_query_lin = rotate(d_query.astype(f32), cosine, -sine_tab).astype(bf16)
    d_second = jnp.where(core == 0, rotate(d_kv, cosine, -sine_tab), d_kv).astype(bf16)

    d_mixed = (dot(d_query_lin, head_q, ROWS) + dot(d_second, head_kv, ROWS)).astype(bf16)
    d_normed = apart(run, scatter_plane, d_mixed)
    d_input_part, gain_one = jax.vjp(rms_scale, inputs, gains[0])[1](d_normed)
    grad_tokens = d_middle + d_input_part

    parts = [dot(normed_all, d_query_lin, FIRST, bf16), dot(normed_all, d_second, FIRST, bf16)]
    parts.append(dot(d_branch_all, heads, FIRST, bf16))
    parts = jnp.stack([part.reshape(line_count * 8, own, HD) for part in parts], axis=1)
    sums = exchange(after(parts, up_back), FINE).reshape(line_count, 8, 3, own, HD)
    sums = jnp.sum(sums.astype(f32), axis=0)
    grad_out = uncolumns(sums[:, 2])
    grad_qkv = sums[:, :2].reshape(KVH, 2, 2, own, HD).transpose(0, 2, 1, 3, 4)
    grad_qkv = uncolumns(lax.optimization_barrier(grad_qkv).reshape(16, own, HD))

    def owned(back):
        return uncolumns(jnp.sum(back.astype(f32), axis=0))

    grad_in = jnp.concatenate([owned(gate_back), owned(up_back)], axis=1)
    grad_down = owned(down_back)

    grad_gains = apart(run, sum_all, jnp.stack([gain_one, gain_two, gain_three, gain_four], axis=0))

    tops = tops.astype(f32) + EPSILON
    qkv_tops = tops[0, :, :, : 4 * HD].reshape(KVH, 2, 2, HD).transpose(0, 2, 1, 3).reshape(-1)
    in_tops = tops[..., 4 * HD :].reshape(8, 2, slice_ff).transpose(1, 0, 2).reshape(-1)
    column_scales = jnp.concatenate([qkv_tops, in_tops], axis=0)
    row_scales = jnp.stack([out_scale, down_scale], axis=0)
    return (
        result,
        grad_tokens,
        grad_qkv,
        grad_out,
        grad_in,
        grad_down,
        grad_gains,
        column_scales,
        row_scales,
    )


def solution(mesh):
    fine = Mesh(
        mesh.devices.reshape(mesh.shape["sp"] // 4, 2, 2, mesh.shape["hd"] // 2, 2), FINE
    )
    split = P(FINE, None)
    in_specs = (split, P(), split, split, split, split, P(), split)
    out_specs = (split, split, split, split, split, split, P(), P(), P(None, FINE))
    return jax.shard_map(
        on_device, mesh=fine, in_specs=in_specs, out_specs=out_specs, check_vma=False
    )
```

```python
import math

import jax
import jax.numpy as jnp
import numpy as np
from jax import lax
from jax.experimental import pallas as pl
from jax.experimental.pallas import tpu as pltpu
from jax.sharding import Mesh
from jax.sharding import PartitionSpec as P

FF = 9216
QH = 8
KVH = 4
HD = 256
WINDOW = 4096

EPSILON = 1e-06
SOFTCAP = 50.0
LEVEL_PULL = 0.75
TWO_PI = 2.0 * math.pi

FINE = ("zh", "zl", "x", "y", "c")
LINE = ("zh", "zl")
PLANE = ("x", "y", "c")
CUBE = ("zl", "x", "y")
SWAP = ((0, 1), (1, 0))

SINE = (
    25.13274115538592,
    -64.83582285607088,
    67.07662736368954,
    -38.49587868201696,
    14.049662842567686,
    -3.16160028673954,
)

f32 = jnp.float32
bf16 = jnp.bfloat16


def sin_turns(turns):
    part = turns - jnp.round(turns)
    square = part * part
    poly = SINE[5]
    for factor in SINE[4::-1]:
        poly = poly * square + factor
    return part * (0.25 - square) * poly


def rms_scale(vector_in, gain_row):
    mean_sq = jnp.mean(vector_in * vector_in, axis=-1, keepdims=True)
    return vector_in * lax.rsqrt(mean_sq + EPSILON) * (1.0 + gain_row)


def nested(weight, channel_scale):
    level = weight * (127.0 / channel_scale)
    level = level - (LEVEL_PULL / TWO_PI) * sin_turns(level)
    four = sin_turns(level * (1.0 / 16.0))
    two = sin_turns(level * (1.0 / 64.0))
    total = 3.0 * level - (16.0 * LEVEL_PULL / TWO_PI) * four - (64.0 * LEVEL_PULL / TWO_PI) * two
    return (channel_scale / 381.0) * total


def rotate(vector_in, cosine, sine_tab):
    half_dim = vector_in.shape[-1] // 2
    first_half = vector_in[..., :half_dim]
    second_half = vector_in[..., half_dim:]
    return jnp.concatenate(
        [
            first_half * cosine - second_half * sine_tab,
            second_half * cosine + first_half * sine_tab,
        ],
        axis=-1,
    )


def rope_tables(position, head_dim):
    half_dim = head_dim // 2
    frequency = np.exp(np.arange(half_dim) * (-2.0 * math.log(10000.0) / head_dim)) / TWO_PI
    coarse = frequency.astype(jnp.bfloat16).astype(np.float32)
    fine = (frequency - coarse).astype(np.float32)
    place = position.astype(f32)[:, None]
    turns = place * coarse[None, :]
    turns = (turns - jnp.round(turns)) + place * fine[None, :]
    return (sin_turns(turns + 0.25), sin_turns(turns))


def doc_info(lengths, places):
    stop_at = jnp.cumsum(lengths, dtype=jnp.int32)
    starts = stop_at - lengths
    inside = starts[None, :] <= places[:, None]
    doc_index = jnp.sum(inside.astype(jnp.int32), axis=1) - 1
    doc_start = jnp.max(jnp.where(inside, starts[None, :], 0), axis=1)
    return (doc_index, places - doc_start)


def glu(gate_in, up_in):
    return jax.nn.gelu(gate_in, approximate=True) * up_in


def dot(left, right, dims, out=f32):
    return lax.dot_general(left, right, (dims, ((), ())), preferred_element_type=out)


ROWS = ((1,), (1,))
COLS = ((1,), (0,))
FIRST = ((0,), (0,))


def swap(value, axis):
    return lax.ppermute(value, axis, SWAP)


def gather_blocks(block, axes, orders, beside=()):
    rows, width = block.shape
    part = width // len(orders)
    parts = []
    for i, order in enumerate(orders):
        held = block[:, i * part : (i + 1) * part].reshape((1,) * len(axes) + (rows, part))
        for axis in order:
            held = jnp.concatenate([held, swap(held, axis)], axis=axes.index(axis))
            if axis == order[0]:
                held = after(held, *beside)
        parts.append(held)
    return jnp.concatenate(parts, axis=-1).reshape(-1, width)


def scatter_blocks(partial, axes, orders, beside=()):
    width = partial.shape[-1]
    part = width // len(orders)
    blocks = partial.reshape((2,) * len(axes) + (-1, width))
    parts = []
    for i, order in enumerate(orders):
        held = blocks[..., i * part : (i + 1) * part]
        for axis in order:
            at = axes.index(axis)
            keep = lax.slice_in_dim(held, 0, 1, axis=at)
            send = lax.slice_in_dim(held, 1, 2, axis=at).astype(bf16)
            come = swap(send, axis)
            if axis == order[0]:
                come = after(come, *beside)
            held = keep.astype(f32) + come.astype(f32)
        parts.append(held.reshape(-1, part))
    return jnp.concatenate(parts, axis=-1)


TOKEN_AXES = ("c", "x", "y")
PLANE_GATHER = (("x", "y", "c"), ("y", "x", "c"))
PLANE_SCATTER = (("c", "y", "x"), ("c", "x", "y"))
CUBE_GATHER = (("zl", "x", "y"), ("x", "y", "zl"), ("y", "zl", "x"))
CUBE_SCATTER = (("y", "x", "zl"), ("zl", "y", "x"), ("x", "zl", "y"))


def after(value, *events):
    return lax.optimization_barrier((value,) + events)[0]


def apart(run, step, *args):
    like = jax.eval_shape(step, *args)

    def nothing(*_):
        return jax.tree.map(lambda leaf: jnp.zeros(leaf.shape, leaf.dtype), like)

    return lax.cond(run, step, nothing, *args)


def both(value, axis):
    other = swap(value, axis)
    first = lax.axis_index(axis) == 0
    return jnp.stack([jnp.where(first, value, other), jnp.where(first, other, value)], axis=0)


def core_sum(grad, own):
    split = grad.reshape(lax.axis_size("zh"), 8, 2, own, grad.shape[-1])
    me = lax.axis_index("c")
    send = lax.dynamic_index_in_dim(split, 1 - me, 2, keepdims=False)
    keep = lax.dynamic_index_in_dim(split, me, 2, keepdims=False)
    return (keep.astype(f32) + swap(send, "c").astype(f32)).astype(bf16)


def line_sum(part):
    flat = part.reshape(-1, part.shape[-1])
    return lax.psum_scatter(flat, "zh", scatter_dimension=0, tiled=True).reshape(part.shape[1:])


def max_both(value, axis):
    return jnp.maximum(value, swap(value, axis))


def sum_all(value):
    for axis in ("c", "x", "y", "zl", "zh"):
        if lax.axis_size(axis) == 2:
            value = value + swap(value, axis)
        else:
            value = lax.psum(value, axis)
    return value


def shift(value, step):
    count = lax.axis_size(LINE)
    return lax.ppermute(value, LINE, [(i, i + step) for i in range(count) if 0 <= i + step < count])


def by_core(part):
    other = swap(part, "c")
    full = jnp.broadcast_to(part[:, :, None], part.shape[:2] + (2,) + part.shape[2:])
    full = lax.dynamic_update_slice_in_dim(full, other[:, :, None], 1 - lax.axis_index("c"), 2)
    return full.reshape(-1, part.shape[-1])


Q_ROWS = 128


def scores(q_ref, k_ref, low_ref, place_ref, k_place_ref):
    raw = dot(q_ref[...], k_ref[...], ROWS) * (1.0 / (math.sqrt(HD) * SOFTCAP))
    places = k_place_ref[...]
    allowed = (places >= low_ref[...]) & (places <= place_ref[...])
    return jnp.tanh(raw), allowed


def attend_kernel(q_ref, k_ref, v_ref, low_ref, place_ref, k_place_ref, out_ref, lse_ref):
    tanh_part, allowed = scores(q_ref, k_ref, low_ref, place_ref, k_place_ref)
    capped = jnp.where(allowed, SOFTCAP * tanh_part, -1e30)
    row_max = jnp.max(capped, axis=1, keepdims=True)
    exp_scores = jnp.exp(capped - row_max)
    row_total = jnp.sum(exp_scores, axis=1, keepdims=True)
    probs = (exp_scores * (1.0 / row_total)).astype(bf16)
    out_ref[...] = dot(probs, v_ref[...], COLS).astype(bf16)
    lse_ref[...] = row_max + jnp.log(row_total)


def attend_back_kernel(
    q_ref, k_ref, v_ref, low_ref, place_ref, k_place_ref, lse_ref, d_ref, dq_ref, dk_ref, dv_ref
):
    @pl.when(pl.program_id(0) == 0)
    def _():
        dk_ref[...] = jnp.zeros_like(dk_ref)
        dv_ref[...] = jnp.zeros_like(dv_ref)

    scale = 1.0 / math.sqrt(HD)
    tanh_part, allowed = scores(q_ref, k_ref, low_ref, place_ref, k_place_ref)
    probs = jnp.where(allowed, jnp.exp(SOFTCAP * tanh_part - lse_ref[...]), 0.0)
    dv_ref[...] += dot(probs.astype(bf16), d_ref[...], FIRST)
    d_prob = dot(d_ref[...], v_ref[...], ROWS)
    delta = jnp.sum(probs * d_prob, axis=1, keepdims=True)
    d_raw = (probs * (d_prob - delta) * (1.0 - tanh_part * tanh_part)).astype(bf16)
    dq_ref[...] = (dot(d_raw, k_ref[...], COLS) * scale).astype(bf16)
    dk_ref[...] += dot(d_raw, q_ref[...], FIRST) * scale


def attention_specs(rows, keys):
    q_spec = pl.BlockSpec((Q_ROWS, HD), lambda i: (i, 0))
    k_spec = pl.BlockSpec((keys, HD), lambda i: (0, 0))
    row_spec = pl.BlockSpec((Q_ROWS, 1), lambda i: (i, 0))
    place_spec = pl.BlockSpec((1, keys), lambda i: (0, 0))
    common = dict(
        grid=(rows // Q_ROWS,),
        compiler_params=pltpu.CompilerParams(
            dimension_semantics=("arbitrary",), vmem_limit_bytes=56 * 2**20
        ),
        cost_estimate=pl.CostEstimate(flops=1, bytes_accessed=1, transcendentals=0),
    )
    return q_spec, k_spec, row_spec, place_spec, common


def attend(query, key_rows, value_rows, low, place, k_place):
    rows, keys = query.shape[0], key_rows.shape[0]
    q_spec, k_spec, row_spec, place_spec, common = attention_specs(rows, keys)
    return pl.pallas_call(
        attend_kernel,
        out_shape=(
            jax.ShapeDtypeStruct((rows, HD), bf16),
            jax.ShapeDtypeStruct((rows, 1), f32),
        ),
        in_specs=[q_spec, k_spec, k_spec, row_spec, row_spec, place_spec],
        out_specs=(q_spec, row_spec),
        **common,
    )(query, key_rows, value_rows, low, place, k_place)


def attend_back(query, key_rows, value_rows, low, place, k_place, lse, d_heads):
    rows, keys = query.shape[0], key_rows.shape[0]
    q_spec, k_spec, row_spec, place_spec, common = attention_specs(rows, keys)
    return pl.pallas_call(
        attend_back_kernel,
        out_shape=(
            jax.ShapeDtypeStruct((rows, HD), bf16),
            jax.ShapeDtypeStruct((keys, HD), f32),
            jax.ShapeDtypeStruct((keys, HD), f32),
        ),
        in_specs=[q_spec, k_spec, k_spec, row_spec, row_spec, place_spec, row_spec, q_spec],
        out_specs=(q_spec, k_spec, k_spec),
        **common,
    )(query, key_rows, value_rows, low, place, k_place, lse, d_heads)


def exchange(value, axes):
    return lax.all_to_all(value, axes, split_axis=0, concat_axis=0, tiled=True)


def columns(weight, count):
    own, width = weight.shape
    return weight.reshape(own, count, width // count).transpose(1, 0, 2)


def uncolumns(parts):
    count, own, width = parts.shape
    return parts.transpose(1, 0, 2).reshape(own, count * width)


def on_device(tokens, gains, w_qkv, w_out, w_in, w_down, lengths, cotangent):
    line_count = lax.axis_size(LINE)
    line_index = lax.axis_index(LINE)
    core = lax.axis_index("c")
    x_index = lax.axis_index("x")
    y_index = lax.axis_index("y")
    tok_rows, model = tokens.shape
    own = w_qkv.shape[0]
    block_rows = 8 * tok_rows
    total_rows = line_count * block_rows
    slice_ff = FF // 8
    run = lengths[0] > 0

    units = lax.optimization_barrier(columns(w_qkv, 16)).reshape(KVH, 2, 2, own, HD)
    qkv_out = units.transpose(0, 2, 1, 3, 4).reshape(8, 2, own, HD)
    qkv_out = jnp.broadcast_to(qkv_out[None], (line_count, 8, 2, own, HD))
    qkv_lat = exchange(qkv_out.reshape(line_count * 8, 2, own, HD), FINE)
    qkv_lat = qkv_lat.reshape(line_count, 8, 2, own, HD)

    inputs = tokens.astype(f32)
    normed = rms_scale(inputs, gains[0]).astype(bf16)
    def gather_plane(block):
        return gather_blocks(block, TOKEN_AXES, PLANE_GATHER)

    def scatter_plane(partial):
        return scatter_blocks(partial, TOKEN_AXES, PLANE_SCATTER)

    def gather_cube(block):
        return gather_blocks(block, CUBE, CUBE_GATHER)

    def scatter_cube(partial):
        return scatter_blocks(partial, CUBE, CUBE_SCATTER)

    normed_all = apart(run, gather_plane, normed)

    out_scale = jnp.max(jnp.abs(w_out.astype(f32)), axis=1) + EPSILON
    down_scale = jnp.max(jnp.abs(w_down.astype(f32)), axis=1) + EPSILON
    eff_out = nested(w_out.astype(f32), out_scale[:, None]).astype(bf16)
    eff_out = jnp.broadcast_to(columns(eff_out, 8)[None], (line_count, 8, own, HD))
    head_out = after(eff_out.reshape(line_count * 8, own, HD), qkv_lat, normed_all)
    head_out = exchange(head_out, FINE)

    def spread(weight):
        cols = jnp.broadcast_to(weight[None], (lax.axis_size("zh"),) + weight.shape)
        return cols.reshape(-1, own, slice_ff)

    def rows_of(sent, *events):
        return exchange(after(sent, *events), LINE + ("x", "y")).reshape(-1, 8, own, slice_ff)

    head_out = head_out.reshape(model, HD)

    qkv_max = jnp.max(jnp.abs(qkv_lat), axis=(0, 1, 3))
    qkv_scale = qkv_max.astype(f32) + EPSILON
    head_qkv = nested(qkv_lat.astype(f32), qkv_scale[None, None, :, None, :]).astype(bf16)
    head_q = head_qkv[:, :, 0].reshape(model, HD)
    head_kv = head_qkv[:, :, 1].reshape(model, HD)

    dev = jnp.arange(8, dtype=jnp.int32)
    dev = (
        ((dev // 2 % 2) ^ x_index) * 4 + ((dev % 2) ^ y_index) * 2 + ((dev // 4) ^ core)
    ).astype(jnp.int32)
    inner = (dev[:, None] * tok_rows + jnp.arange(tok_rows, dtype=jnp.int32)[None, :]).reshape(-1)
    q_places = line_index * block_rows + inner
    position = doc_info(lengths, q_places)[1]
    cosine, sine_tab = rope_tables(position, HD)

    second = dot(normed_all, head_kv, COLS)
    kv_own = jnp.where(core == 0, rotate(second, cosine, sine_tab), second).astype(bf16)

    reach = min(WINDOW, total_rows // 2)
    back = min(line_count - 1, -(-(reach - 1) // block_rows))
    half_block = block_rows // 2

    def flip(value):
        return jnp.concatenate([value[:, half_block:], value[:, :half_block]], axis=1)

    def pass_up(own_rows, normed_all, head_q, cosine, sine_tab, w_in):
        query = rotate(dot(normed_all, head_q, COLS), cosine, sine_tab).astype(bf16)
        sent = spread(columns(w_in[:, :FF], 8))
        shifted = [own_rows]
        for _ in range(back):
            shifted.append(after(shift(shifted[-1], 1), query, sent))
        mine = jnp.stack(shifted[::-1], axis=0)
        other = flip(swap(mine, "c"))
        keys = jnp.where(core == 0, mine, other).reshape(-1, HD)
        values = jnp.where(core == 0, other, mine).reshape(-1, HD)
        return keys, values, query, sent

    key_rows, value_rows, query, gate_sent = apart(
        run, pass_up, kv_own, normed_all, head_q, cosine, sine_tab, w_in
    )

    gate_lat = rows_of(gate_sent, head_out, key_rows)
    def quantize(lat):
        top = max_both(jnp.max(jnp.abs(lat), axis=(0, 1, 2)), "c")
        return top, nested(lat.astype(f32), top.astype(f32) + EPSILON).astype(bf16)

    k_places = jnp.concatenate(
        [q_places - n * block_rows for n in range(back, -1, -1)], axis=0
    )
    place = q_places[:, None]
    low = jnp.maximum(q_places - position, q_places - (WINDOW - 1))[:, None]
    heads, lse = attend(query, key_rows, value_rows, low, place, k_places[None])

    branch = dot(heads, head_out, ROWS, bf16)


    def scatter_branch(partial, w_in):
        sent = spread(columns(w_in[:, FF:], 8))
        return scatter_blocks(partial, TOKEN_AXES, PLANE_SCATTER, (sent,)), sent

    branch, up_sent = apart(run, scatter_branch, branch, w_in)
    up_lat = rows_of(up_sent, gate_lat, branch)
    middle = inputs + rms_scale(branch, gains[1])
    pre_mlp = rms_scale(middle, gains[2]).astype(bf16)

    def gather_pre(block, lat, w_down, down_scale):
        top, low = quantize(lat)
        eff_down = nested(w_down.astype(f32), down_scale[:, None]).astype(bf16)
        down_sent = spread(columns(eff_down, 8))
        tokens_all = gather_blocks(block, CUBE, CUBE_GATHER, (low, down_sent))
        return tokens_all, top, by_core(low), down_sent

    pre_all, gate_top, cols_gate, down_sent = apart(
        run, gather_pre, pre_mlp, gate_lat, w_down, down_scale
    )
    down_lat = rows_of(down_sent, up_lat, pre_all)

    def effective(lat):
        top, low = quantize(lat)
        return top, by_core(low)

    up_top, cols_up = apart(run, effective, after(up_lat, cols_gate))
    in_tops = jnp.concatenate([gate_top, up_top])
    pre_turned = lax.optimization_barrier(pre_all.T)
    gate_part = dot(pre_all, cols_gate, COLS)
    up_part = dot(pre_all, cols_up, COLS)
    cols_down = apart(run, by_core, after(down_lat, gate_part, up_part))
    hidden = glu(gate_part, up_part).astype(bf16)
    down_out = apart(run, scatter_cube, dot(hidden, cols_down, ROWS, bf16))
    result = (middle + rms_scale(down_out, gains[3])).astype(bf16)

    grad_result = cotangent.astype(f32)
    d_down, gain_four = jax.vjp(rms_scale, down_out, gains[3])[1](grad_result)
    d_down = d_down.astype(bf16)

    def gather_down(block, qkv_row, in_row):
        tops = jnp.concatenate([both(qkv_row, "c").reshape(-1), in_row], axis=0)
        return gather_cube(block), both(both(both(tops, "y"), "x"), "zl")

    d_down_all, tops = apart(
        run, gather_down, d_down, qkv_max.reshape(-1), in_tops
    )

    def hidden_back(d_down_all, hidden, gate_part, up_part, cols_down):
        part = dot(d_down_all, hidden, FIRST, bf16)
        d_hidden = dot(after(d_down_all, part), cols_down, COLS)
        d_gate, d_up = jax.vjp(glu, gate_part, up_part)[1](d_hidden)
        return core_sum(part, own), d_gate.astype(bf16), d_up.astype(bf16)

    part_down, d_gate, d_up = apart(
        run, hidden_back, d_down_all, hidden, gate_part, up_part, cols_down
    )

    def collect(part, *events):
        flat = after(part.reshape(-1, own, slice_ff), *events)
        return exchange(flat, LINE + ("x", "y")).reshape(-1, 8, own, slice_ff)

    down_back = collect(part_down)
    d_pre = (dot(d_gate, cols_gate, ROWS) + dot(d_up, cols_up, ROWS)).astype(bf16)

    def scatter_pre(partial, pre_turned, d_gate, d_up):
        gate = dot(pre_turned, d_gate, COLS, bf16)
        up = dot(pre_turned, d_up, COLS, bf16)
        total = scatter_blocks(partial, CUBE, CUBE_SCATTER, (gate, up))
        return total, core_sum(gate, own), core_sum(up, own)

    d_pre, part_gate, part_up = apart(run, scatter_pre, d_pre, pre_turned, d_gate, d_up)
    gate_back = collect(part_gate, down_back)
    d_mid_part, gain_three = jax.vjp(rms_scale, middle, gains[2])[1](d_pre)
    d_middle = grad_result + d_mid_part
    d_branch, gain_two = jax.vjp(rms_scale, branch, gains[1])[1](d_middle)
    d_branch_all = apart(run, gather_plane, d_branch.astype(bf16))
    up_back = collect(part_up, gate_back, d_branch_all)
    d_heads = dot(d_branch_all, head_out, COLS).astype(bf16)

    d_query, d_keys, d_values = attend_back(
        query, key_rows, value_rows, low, place, k_places[None], lse, d_heads
    )

    def pass_down(d_keys, d_values, d_branch_all, heads, normed_all):
        part_out = dot(d_branch_all, heads, FIRST, bf16)
        normed_turned = lax.optimization_barrier(normed_all.T)
        d_keys = d_keys.reshape(back + 1, block_rows, HD)
        d_values = d_values.reshape(back + 1, block_rows, HD)
        send = flip(jnp.where(core == 0, d_values, d_keys).astype(bf16))
        window = jnp.where(core == 0, d_keys, d_values) + swap(send, "c").astype(f32)
        total = window[0]
        for n in range(1, back + 1):
            come = shift(total.astype(bf16), -1)
            total = window[n] + after(come, part_out, normed_turned).astype(f32)
        return total.astype(bf16), part_out, normed_turned

    d_kv, part_out, normed_turned = apart(
        run, pass_down, d_keys, d_values, d_branch_all, heads, normed_all
    )
    d_kv = d_kv.astype(f32)
    d_query_lin = rotate(d_query.astype(f32), cosine, -sine_tab).astype(bf16)
    d_second = jnp.where(core == 0, rotate(d_kv, cosine, -sine_tab), d_kv).astype(bf16)

    d_mixed = (dot(d_query_lin, head_q, ROWS) + dot(d_second, head_kv, ROWS)).astype(bf16)
    d_normed = apart(run, scatter_plane, d_mixed)
    d_input_part, gain_one = jax.vjp(rms_scale, inputs, gains[0])[1](d_normed)
    grad_tokens = d_middle + d_input_part

    parts = [dot(normed_turned, d_query_lin, COLS, bf16), dot(normed_turned, d_second, COLS, bf16)]
    parts.append(part_out)
    parts = jnp.stack([part.reshape(line_count * 8, own, HD) for part in parts], axis=1)
    sums = exchange(after(parts, up_back), FINE).reshape(line_count, 8, 3, own, HD)
    sums = jnp.sum(sums.astype(f32), axis=0)
    grad_out = uncolumns(sums[:, 2])
    grad_qkv = sums[:, :2].reshape(KVH, 2, 2, own, HD).transpose(0, 2, 1, 3, 4)
    grad_qkv = uncolumns(lax.optimization_barrier(grad_qkv).reshape(16, own, HD))

    def owned(back):
        return uncolumns(jnp.sum(back.astype(f32), axis=0))

    grad_in = jnp.concatenate([owned(gate_back), owned(up_back)], axis=1)
    grad_down = owned(down_back)

    grad_gains = apart(run, sum_all, jnp.stack([gain_one, gain_two, gain_three, gain_four], axis=0))

    tops = tops.astype(f32) + EPSILON
    qkv_tops = tops[0, :, :, : 4 * HD].reshape(KVH, 2, 2, HD).transpose(0, 2, 1, 3).reshape(-1)
    in_tops = tops[..., 4 * HD :].reshape(8, 2, slice_ff).transpose(1, 0, 2).reshape(-1)
    column_scales = jnp.concatenate([qkv_tops, in_tops], axis=0)
    row_scales = jnp.stack([out_scale, down_scale], axis=0)
    return (
        result,
        grad_tokens,
        grad_qkv,
        grad_out,
        grad_in,
        grad_down,
        grad_gains,
        column_scales,
        row_scales,
    )


def solution(mesh):
    fine = Mesh(
        mesh.devices.reshape(mesh.shape["sp"] // 4, 2, 2, mesh.shape["hd"] // 2, 2), FINE
    )
    split = P(FINE, None)
    in_specs = (split, P(), split, split, split, split, P(), split)
    out_specs = (split, split, split, split, split, split, P(), P(), P(None, FINE))
    return jax.shard_map(
        on_device, mesh=fine, in_specs=in_specs, out_specs=out_specs, check_vma=False
    )
```

```python
import math

import jax
import jax.numpy as jnp
import numpy as np
from jax import lax
from jax.experimental import pallas as pl
from jax.experimental.pallas import tpu as pltpu
from jax.sharding import Mesh
from jax.sharding import PartitionSpec as P

FF = 9216
QH = 8
KVH = 4
HD = 256
WINDOW = 4096

EPSILON = 1e-06
SOFTCAP = 50.0
LEVEL_PULL = 0.75
TWO_PI = 2.0 * math.pi

FINE = ("zh", "zl", "x", "y", "c")
LINE = ("zh", "zl")
PLANE = ("x", "y", "c")
CUBE = ("zl", "x", "y")
SWAP = ((0, 1), (1, 0))

SINE = (
    25.13274115538592,
    -64.83582285607088,
    67.07662736368954,
    -38.49587868201696,
    14.049662842567686,
    -3.16160028673954,
)

f32 = jnp.float32
bf16 = jnp.bfloat16


def sin_turns(turns):
    part = turns - jnp.round(turns)
    square = part * part
    poly = SINE[5]
    for factor in SINE[4::-1]:
        poly = poly * square + factor
    return part * (0.25 - square) * poly


def rms_scale(vector_in, gain_row):
    mean_sq = jnp.mean(vector_in * vector_in, axis=-1, keepdims=True)
    return vector_in * lax.rsqrt(mean_sq + EPSILON) * (1.0 + gain_row)


def nested(weight, channel_scale):
    level = weight * (127.0 / channel_scale)
    level = level - (LEVEL_PULL / TWO_PI) * sin_turns(level)
    four = sin_turns(level * (1.0 / 16.0))
    two = sin_turns(level * (1.0 / 64.0))
    total = 3.0 * level - (16.0 * LEVEL_PULL / TWO_PI) * four - (64.0 * LEVEL_PULL / TWO_PI) * two
    return (channel_scale / 381.0) * total


def rotate(vector_in, cosine, sine_tab):
    half_dim = vector_in.shape[-1] // 2
    first_half = vector_in[..., :half_dim]
    second_half = vector_in[..., half_dim:]
    return jnp.concatenate(
        [
            first_half * cosine - second_half * sine_tab,
            second_half * cosine + first_half * sine_tab,
        ],
        axis=-1,
    )


def rope_tables(position, head_dim):
    half_dim = head_dim // 2
    frequency = np.exp(np.arange(half_dim) * (-2.0 * math.log(10000.0) / head_dim)) / TWO_PI
    coarse = frequency.astype(jnp.bfloat16).astype(np.float32)
    fine = (frequency - coarse).astype(np.float32)
    place = position.astype(f32)[:, None]
    turns = place * coarse[None, :]
    turns = (turns - jnp.round(turns)) + place * fine[None, :]
    return (sin_turns(turns + 0.25), sin_turns(turns))


def doc_info(lengths, places):
    stop_at = jnp.cumsum(lengths, dtype=jnp.int32)
    starts = stop_at - lengths
    inside = starts[None, :] <= places[:, None]
    doc_index = jnp.sum(inside.astype(jnp.int32), axis=1) - 1
    doc_start = jnp.max(jnp.where(inside, starts[None, :], 0), axis=1)
    return (doc_index, places - doc_start)


def glu(gate_in, up_in):
    return jax.nn.gelu(gate_in, approximate=True) * up_in


def dot(left, right, dims, out=f32):
    return lax.dot_general(left, right, (dims, ((), ())), preferred_element_type=out)


ROWS = ((1,), (1,))
COLS = ((1,), (0,))
FIRST = ((0,), (0,))


def swap(value, axis):
    return lax.ppermute(value, axis, SWAP)


def gather_blocks(block, axes, orders, beside=()):
    rows, width = block.shape
    part = width // len(orders)
    parts = []
    for i, order in enumerate(orders):
        held = block[:, i * part : (i + 1) * part].reshape((1,) * len(axes) + (rows, part))
        for axis in order:
            held = jnp.concatenate([held, swap(held, axis)], axis=axes.index(axis))
            if axis == order[0]:
                held = after(held, *beside)
        parts.append(held)
    return jnp.concatenate(parts, axis=-1).reshape(-1, width)


def scatter_blocks(partial, axes, orders, beside=()):
    width = partial.shape[-1]
    part = width // len(orders)
    blocks = partial.reshape((2,) * len(axes) + (-1, width))
    parts = []
    for i, order in enumerate(orders):
        held = blocks[..., i * part : (i + 1) * part]
        for axis in order:
            at = axes.index(axis)
            keep = lax.slice_in_dim(held, 0, 1, axis=at)
            send = lax.slice_in_dim(held, 1, 2, axis=at).astype(bf16)
            come = swap(send, axis)
            if axis == order[0]:
                come = after(come, *beside)
            held = keep.astype(f32) + come.astype(f32)
        parts.append(held.reshape(-1, part))
    return jnp.concatenate(parts, axis=-1)


TOKEN_AXES = ("c", "x", "y")
PLANE_GATHER = (("x", "y", "c"), ("y", "x", "c"))
PLANE_SCATTER = (("c", "y", "x"), ("c", "x", "y"))
CUBE_GATHER = (("zl", "x", "y"), ("x", "y", "zl"), ("y", "zl", "x"))
CUBE_SCATTER = (("y", "x", "zl"), ("zl", "y", "x"), ("x", "zl", "y"))


def after(value, *events):
    return lax.optimization_barrier((value,) + events)[0]


def apart(run, step, *args):
    like = jax.eval_shape(step, *args)

    def nothing(*_):
        return jax.tree.map(lambda leaf: jnp.zeros(leaf.shape, leaf.dtype), like)

    return lax.cond(run, step, nothing, *args)


def both(value, axis):
    other = swap(value, axis)
    first = lax.axis_index(axis) == 0
    return jnp.stack([jnp.where(first, value, other), jnp.where(first, other, value)], axis=0)


def core_sum(grad, own):
    split = grad.reshape(lax.axis_size("zh"), 8, 2, own, grad.shape[-1])
    me = lax.axis_index("c")
    send = lax.dynamic_index_in_dim(split, 1 - me, 2, keepdims=False)
    keep = lax.dynamic_index_in_dim(split, me, 2, keepdims=False)
    return (keep.astype(f32) + swap(send, "c").astype(f32)).astype(bf16)


def line_sum(part):
    flat = part.reshape(-1, part.shape[-1])
    return lax.psum_scatter(flat, "zh", scatter_dimension=0, tiled=True).reshape(part.shape[1:])


def max_both(value, axis):
    return jnp.maximum(value, swap(value, axis))


def sum_all(value):
    for axis in ("c", "x", "y", "zl", "zh"):
        if lax.axis_size(axis) == 2:
            value = value + swap(value, axis)
        else:
            value = lax.psum(value, axis)
    return value


def shift(value, step):
    count = lax.axis_size(LINE)
    return lax.ppermute(value, LINE, [(i, i + step) for i in range(count) if 0 <= i + step < count])


def by_core(part):
    other = swap(part, "c")
    full = jnp.broadcast_to(part[:, :, None], part.shape[:2] + (2,) + part.shape[2:])
    full = lax.dynamic_update_slice_in_dim(full, other[:, :, None], 1 - lax.axis_index("c"), 2)
    return full.reshape(-1, part.shape[-1])


def scores(q_ref, k_ref, low_ref, place_ref, k_place_ref):
    raw = dot(q_ref[...], k_ref[...], ROWS) * (1.0 / (math.sqrt(HD) * SOFTCAP))
    places = k_place_ref[...]
    allowed = (places >= low_ref[...]) & (places <= place_ref[...])
    return jnp.tanh(raw), allowed


def attend_kernel(q_ref, k_ref, v_ref, low_ref, place_ref, k_place_ref, out_ref, lse_ref):
    tanh_part, allowed = scores(q_ref, k_ref, low_ref, place_ref, k_place_ref)
    capped = jnp.where(allowed, SOFTCAP * tanh_part, -1e30)
    row_max = jnp.max(capped, axis=1, keepdims=True)
    exp_scores = jnp.exp(capped - row_max)
    row_total = jnp.sum(exp_scores, axis=1, keepdims=True)
    probs = (exp_scores * (1.0 / row_total)).astype(bf16)
    out_ref[...] = dot(probs, v_ref[...], COLS).astype(bf16)
    lse_ref[...] = row_max + jnp.log(row_total)


def attend_back_kernel(
    q_ref, k_ref, v_ref, low_ref, place_ref, k_place_ref, lse_ref, d_ref, dq_ref, dk_ref, dv_ref
):
    @pl.when(pl.program_id(0) == 0)
    def _():
        dk_ref[...] = jnp.zeros_like(dk_ref)
        dv_ref[...] = jnp.zeros_like(dv_ref)

    scale = 1.0 / math.sqrt(HD)
    tanh_part, allowed = scores(q_ref, k_ref, low_ref, place_ref, k_place_ref)
    probs = jnp.where(allowed, jnp.exp(SOFTCAP * tanh_part - lse_ref[...]), 0.0)
    dv_ref[...] += dot(probs.astype(bf16), d_ref[...], FIRST)
    d_prob = dot(d_ref[...], v_ref[...], ROWS)
    delta = jnp.sum(probs * d_prob, axis=1, keepdims=True)
    d_raw = (probs * (d_prob - delta) * (1.0 - tanh_part * tanh_part)).astype(bf16)
    dq_ref[...] = (dot(d_raw, k_ref[...], COLS) * scale).astype(bf16)
    dk_ref[...] += dot(d_raw, q_ref[...], FIRST) * scale


def attention_specs(rows, keys):
    q_rows = 256 if keys <= 4096 else 128
    q_spec = pl.BlockSpec((q_rows, HD), lambda i: (i, 0))
    k_spec = pl.BlockSpec((keys, HD), lambda i: (0, 0))
    row_spec = pl.BlockSpec((q_rows, 1), lambda i: (i, 0))
    place_spec = pl.BlockSpec((1, keys), lambda i: (0, 0))
    common = dict(
        grid=(rows // q_rows,),
        compiler_params=pltpu.CompilerParams(
            dimension_semantics=("arbitrary",), vmem_limit_bytes=56 * 2**20
        ),
        cost_estimate=pl.CostEstimate(flops=1, bytes_accessed=1, transcendentals=0),
    )
    return q_spec, k_spec, row_spec, place_spec, common


def attend(query, key_rows, value_rows, low, place, k_place):
    rows, keys = query.shape[0], key_rows.shape[0]
    q_spec, k_spec, row_spec, place_spec, common = attention_specs(rows, keys)
    return pl.pallas_call(
        attend_kernel,
        out_shape=(
            jax.ShapeDtypeStruct((rows, HD), bf16),
            jax.ShapeDtypeStruct((rows, 1), f32),
        ),
        in_specs=[q_spec, k_spec, k_spec, row_spec, row_spec, place_spec],
        out_specs=(q_spec, row_spec),
        **common,
    )(query, key_rows, value_rows, low, place, k_place)


def attend_back(query, key_rows, value_rows, low, place, k_place, lse, d_heads):
    rows, keys = query.shape[0], key_rows.shape[0]
    q_spec, k_spec, row_spec, place_spec, common = attention_specs(rows, keys)
    return pl.pallas_call(
        attend_back_kernel,
        out_shape=(
            jax.ShapeDtypeStruct((rows, HD), bf16),
            jax.ShapeDtypeStruct((keys, HD), f32),
            jax.ShapeDtypeStruct((keys, HD), f32),
        ),
        in_specs=[q_spec, k_spec, k_spec, row_spec, row_spec, place_spec, row_spec, q_spec],
        out_specs=(q_spec, k_spec, k_spec),
        **common,
    )(query, key_rows, value_rows, low, place, k_place, lse, d_heads)


def exchange(value, axes):
    return lax.all_to_all(value, axes, split_axis=0, concat_axis=0, tiled=True)


def columns(weight, count):
    own, width = weight.shape
    return weight.reshape(own, count, width // count).transpose(1, 0, 2)


def uncolumns(parts):
    count, own, width = parts.shape
    return parts.transpose(1, 0, 2).reshape(own, count * width)


def on_device(tokens, gains, w_qkv, w_out, w_in, w_down, lengths, cotangent):
    line_count = lax.axis_size(LINE)
    line_index = lax.axis_index(LINE)
    core = lax.axis_index("c")
    x_index = lax.axis_index("x")
    y_index = lax.axis_index("y")
    tok_rows, model = tokens.shape
    own = w_qkv.shape[0]
    block_rows = 8 * tok_rows
    total_rows = line_count * block_rows
    slice_ff = FF // 8
    run = lengths[0] > 0

    units = lax.optimization_barrier(columns(w_qkv, 16)).reshape(KVH, 2, 2, own, HD)
    qkv_out = units.transpose(0, 2, 1, 3, 4).reshape(8, 2, own, HD)
    qkv_out = jnp.broadcast_to(qkv_out[None], (line_count, 8, 2, own, HD))
    qkv_lat = exchange(qkv_out.reshape(line_count * 8, 2, own, HD), FINE)
    qkv_lat = qkv_lat.reshape(line_count, 8, 2, own, HD)

    inputs = tokens.astype(f32)
    normed = rms_scale(inputs, gains[0]).astype(bf16)
    def gather_plane(block):
        return gather_blocks(block, TOKEN_AXES, PLANE_GATHER)

    def scatter_plane(partial):
        return scatter_blocks(partial, TOKEN_AXES, PLANE_SCATTER)

    def gather_cube(block):
        return gather_blocks(block, CUBE, CUBE_GATHER)

    def scatter_cube(partial):
        return scatter_blocks(partial, CUBE, CUBE_SCATTER)

    normed_all = apart(run, gather_plane, normed)

    out_scale = jnp.max(jnp.abs(w_out.astype(f32)), axis=1) + EPSILON
    down_scale = jnp.max(jnp.abs(w_down.astype(f32)), axis=1) + EPSILON
    eff_out = nested(w_out.astype(f32), out_scale[:, None]).astype(bf16)
    eff_out = jnp.broadcast_to(columns(eff_out, 8)[None], (line_count, 8, own, HD))
    head_out = after(eff_out.reshape(line_count * 8, own, HD), qkv_lat, normed_all)
    head_out = exchange(head_out, FINE)

    def spread(weight):
        cols = jnp.broadcast_to(weight[None], (lax.axis_size("zh"),) + weight.shape)
        return cols.reshape(-1, own, slice_ff)

    def rows_of(sent, *events):
        return exchange(after(sent, *events), LINE + ("x", "y")).reshape(-1, 8, own, slice_ff)

    head_out = head_out.reshape(model, HD)

    qkv_max = jnp.max(jnp.abs(qkv_lat), axis=(0, 1, 3))
    qkv_scale = qkv_max.astype(f32) + EPSILON
    head_qkv = nested(qkv_lat.astype(f32), qkv_scale[None, None, :, None, :]).astype(bf16)
    head_q = head_qkv[:, :, 0].reshape(model, HD)
    head_kv = head_qkv[:, :, 1].reshape(model, HD)

    dev = jnp.arange(8, dtype=jnp.int32)
    dev = (
        ((dev // 2 % 2) ^ x_index) * 4 + ((dev % 2) ^ y_index) * 2 + ((dev // 4) ^ core)
    ).astype(jnp.int32)
    inner = (dev[:, None] * tok_rows + jnp.arange(tok_rows, dtype=jnp.int32)[None, :]).reshape(-1)
    q_places = line_index * block_rows + inner
    position = doc_info(lengths, q_places)[1]
    cosine, sine_tab = rope_tables(position, HD)

    second = dot(normed_all, head_kv, COLS)
    kv_own = jnp.where(core == 0, rotate(second, cosine, sine_tab), second).astype(bf16)

    reach = min(WINDOW, total_rows // 2)
    back = min(line_count - 1, -(-(reach - 1) // block_rows))
    half_block = block_rows // 2

    def flip(value):
        return jnp.concatenate([value[:, half_block:], value[:, :half_block]], axis=1)

    def pass_up(own_rows, normed_all, head_q, cosine, sine_tab, w_in):
        query = rotate(dot(normed_all, head_q, COLS), cosine, sine_tab).astype(bf16)
        sent = spread(columns(w_in[:, :FF], 8))
        shifted = [own_rows]
        for _ in range(back):
            shifted.append(after(shift(shifted[-1], 1), query, sent))
        mine = jnp.stack(shifted[::-1], axis=0)
        other = flip(swap(mine, "c"))
        keys = jnp.where(core == 0, mine, other).reshape(-1, HD)
        values = jnp.where(core == 0, other, mine).reshape(-1, HD)
        return keys, values, query, sent

    key_rows, value_rows, query, gate_sent = apart(
        run, pass_up, kv_own, normed_all, head_q, cosine, sine_tab, w_in
    )

    gate_lat = rows_of(gate_sent, head_out, key_rows)
    def quantize(lat):
        top = max_both(jnp.max(jnp.abs(lat), axis=(0, 1, 2)), "c")
        return top, nested(lat.astype(f32), top.astype(f32) + EPSILON).astype(bf16)

    k_places = jnp.concatenate(
        [q_places - n * block_rows for n in range(back, -1, -1)], axis=0
    )
    place = q_places[:, None]
    low = jnp.maximum(q_places - position, q_places - (WINDOW - 1))[:, None]
    heads, lse = attend(query, key_rows, value_rows, low, place, k_places[None])

    branch = dot(heads, head_out, ROWS, bf16)


    def scatter_branch(partial, w_in):
        sent = spread(columns(w_in[:, FF:], 8))
        return scatter_blocks(partial, TOKEN_AXES, PLANE_SCATTER, (sent,)), sent

    branch, up_sent = apart(run, scatter_branch, branch, w_in)
    up_lat = rows_of(up_sent, gate_lat, branch)
    middle = inputs + rms_scale(branch, gains[1])
    pre_mlp = rms_scale(middle, gains[2]).astype(bf16)

    def gather_pre(block, lat, w_down, down_scale):
        top, low = quantize(lat)
        eff_down = nested(w_down.astype(f32), down_scale[:, None]).astype(bf16)
        down_sent = spread(columns(eff_down, 8))
        tokens_all = gather_blocks(block, CUBE, CUBE_GATHER, (low, down_sent))
        return tokens_all, top, by_core(low), down_sent

    pre_all, gate_top, cols_gate, down_sent = apart(
        run, gather_pre, pre_mlp, gate_lat, w_down, down_scale
    )
    down_lat = rows_of(down_sent, up_lat, pre_all)

    def effective(lat):
        top, low = quantize(lat)
        return top, by_core(low)

    up_top, cols_up = apart(run, effective, after(up_lat, cols_gate))
    in_tops = jnp.concatenate([gate_top, up_top])
    pre_turned = lax.optimization_barrier(pre_all.T)
    gate_part = dot(pre_all, cols_gate, COLS)
    up_part = dot(pre_all, cols_up, COLS)
    cols_down = apart(run, by_core, after(down_lat, gate_part, up_part))
    hidden = glu(gate_part, up_part).astype(bf16)
    down_out = apart(run, scatter_cube, dot(hidden, cols_down, ROWS, bf16))
    result = (middle + rms_scale(down_out, gains[3])).astype(bf16)

    grad_result = cotangent.astype(f32)
    d_down, gain_four = jax.vjp(rms_scale, down_out, gains[3])[1](grad_result)
    d_down = d_down.astype(bf16)

    def gather_down(block, qkv_row, in_row):
        tops = jnp.concatenate([both(qkv_row, "c").reshape(-1), in_row], axis=0)
        return gather_cube(block), both(both(both(tops, "y"), "x"), "zl")

    d_down_all, tops = apart(
        run, gather_down, d_down, qkv_max.reshape(-1), in_tops
    )

    def hidden_back(d_down_all, hidden, gate_part, up_part, cols_down):
        part = dot(d_down_all, hidden, FIRST, bf16)
        d_hidden = dot(after(d_down_all, part), cols_down, COLS)
        d_gate, d_up = jax.vjp(glu, gate_part, up_part)[1](d_hidden)
        return core_sum(part, own), d_gate.astype(bf16), d_up.astype(bf16)

    part_down, d_gate, d_up = apart(
        run, hidden_back, d_down_all, hidden, gate_part, up_part, cols_down
    )

    def collect(part, *events):
        flat = after(part.reshape(-1, own, slice_ff), *events)
        return exchange(flat, LINE + ("x", "y")).reshape(-1, 8, own, slice_ff)

    down_back = collect(part_down)
    d_pre = (dot(d_gate, cols_gate, ROWS) + dot(d_up, cols_up, ROWS)).astype(bf16)

    def scatter_pre(partial, pre_turned, d_gate, d_up):
        gate = dot(pre_turned, d_gate, COLS, bf16)
        up = dot(pre_turned, d_up, COLS, bf16)
        total = scatter_blocks(partial, CUBE, CUBE_SCATTER, (gate, up))
        return total, core_sum(gate, own), core_sum(up, own)

    d_pre, part_gate, part_up = apart(run, scatter_pre, d_pre, pre_turned, d_gate, d_up)
    gate_back = collect(part_gate, down_back)
    d_mid_part, gain_three = jax.vjp(rms_scale, middle, gains[2])[1](d_pre)
    d_middle = grad_result + d_mid_part
    d_branch, gain_two = jax.vjp(rms_scale, branch, gains[1])[1](d_middle)
    d_branch_all = apart(run, gather_plane, d_branch.astype(bf16))
    up_back = collect(part_up, gate_back, d_branch_all)
    d_heads = dot(d_branch_all, head_out, COLS).astype(bf16)

    d_query, d_keys, d_values = attend_back(
        query, key_rows, value_rows, low, place, k_places[None], lse, d_heads
    )

    def pass_down(d_keys, d_values, d_branch_all, heads, normed_all):
        part_out = dot(d_branch_all, heads, FIRST, bf16)
        normed_turned = lax.optimization_barrier(normed_all.T)
        d_keys = d_keys.reshape(back + 1, block_rows, HD)
        d_values = d_values.reshape(back + 1, block_rows, HD)
        send = flip(jnp.where(core == 0, d_values, d_keys).astype(bf16))
        window = jnp.where(core == 0, d_keys, d_values) + swap(send, "c").astype(f32)
        total = window[0]
        for n in range(1, back + 1):
            come = shift(total.astype(bf16), -1)
            total = window[n] + after(come, part_out, normed_turned).astype(f32)
        return total.astype(bf16), part_out, normed_turned

    d_kv, part_out, normed_turned = apart(
        run, pass_down, d_keys, d_values, d_branch_all, heads, normed_all
    )
    d_kv = d_kv.astype(f32)
    d_query_lin = rotate(d_query.astype(f32), cosine, -sine_tab).astype(bf16)
    d_second = jnp.where(core == 0, rotate(d_kv, cosine, -sine_tab), d_kv).astype(bf16)

    d_mixed = (dot(d_query_lin, head_q, ROWS) + dot(d_second, head_kv, ROWS)).astype(bf16)
    d_normed = apart(run, scatter_plane, d_mixed)
    d_input_part, gain_one = jax.vjp(rms_scale, inputs, gains[0])[1](d_normed)
    grad_tokens = d_middle + d_input_part

    parts = [dot(normed_turned, d_query_lin, COLS, bf16), dot(normed_turned, d_second, COLS, bf16)]
    parts.append(part_out)
    parts = jnp.stack([part.reshape(line_count * 8, own, HD) for part in parts], axis=1)
    sums = exchange(after(parts, up_back), FINE).reshape(line_count, 8, 3, own, HD)
    sums = jnp.sum(sums.astype(f32), axis=0)
    grad_out = uncolumns(sums[:, 2])
    grad_qkv = sums[:, :2].reshape(KVH, 2, 2, own, HD).transpose(0, 2, 1, 3, 4)
    grad_qkv = uncolumns(lax.optimization_barrier(grad_qkv).reshape(16, own, HD))

    def owned(back):
        return uncolumns(jnp.sum(back.astype(f32), axis=0))

    grad_in = jnp.concatenate([owned(gate_back), owned(up_back)], axis=1)
    grad_down = owned(down_back)

    grad_gains = apart(run, sum_all, jnp.stack([gain_one, gain_two, gain_three, gain_four], axis=0))

    tops = tops.astype(f32) + EPSILON
    qkv_tops = tops[0, :, :, : 4 * HD].reshape(KVH, 2, 2, HD).transpose(0, 2, 1, 3).reshape(-1)
    in_tops = tops[..., 4 * HD :].reshape(8, 2, slice_ff).transpose(1, 0, 2).reshape(-1)
    column_scales = jnp.concatenate([qkv_tops, in_tops], axis=0)
    row_scales = jnp.stack([out_scale, down_scale], axis=0)
    return (
        result,
        grad_tokens,
        grad_qkv,
        grad_out,
        grad_in,
        grad_down,
        grad_gains,
        column_scales,
        row_scales,
    )


def solution(mesh):
    fine = Mesh(
        mesh.devices.reshape(mesh.shape["sp"] // 4, 2, 2, mesh.shape["hd"] // 2, 2), FINE
    )
    split = P(FINE, None)
    in_specs = (split, P(), split, split, split, split, P(), split)
    out_specs = (split, split, split, split, split, split, P(), P(), P(None, FINE))
    return jax.shard_map(
        on_device, mesh=fine, in_specs=in_specs, out_specs=out_specs, check_vma=False
    )
```
